512 devices in a mesh: blk: 8 (over x, core), pair: 2 (over y_lo), dp: 32 (over y_hi, z).
Axes of the slice: x: 4, y: 4 (y_hi: 2, y_lo: 2; y = y_hi * 2 + y_lo), z: 16, core: 2. Of those that a mesh axis runs over, the one named last changes fastest.
Arguments:
- acts: bfloat16 [4096, 8192], P('dp'), may hold values from -6 to 6
- grads: bfloat16 [4096, 8192], P('dp'), may hold values from -1.5 to 1.5
- basis_in: float32 [8192, 4096], P('dp', ('blk', 'pair')), may hold values from -0.0625 to 0.0625
- basis_out: float32 [8192, 4096], P('dp', ('blk', 'pair')), may hold values from -0.0625 to 0.0625
- seq_ids: int32 [4096], P('dp'), may hold values from 0 to 127, as said below
Outputs:
- eig_scale: float32 [4096, 4096], P(('blk', 'pair'), 'dp')
The draws below stay inside these ranges and needn't reach their ends.
Inputs may be any that keep to these rules, and one draw needn't show every extreme that they name: seq_ids never fall along the tokens; the 128 tokens of index k of dp carry exactly the ids k * 4 to k * 4 + 3, each at least once.
All inputs are finite; a program needn't handle non-finite values.
Results may differ from the reference program's by a relative error of at most 0.0017.
Values may be sent and summed in bfloat16 or wider, within the bound.
A program may use at most 64 MiB of HBM per device.

```python
import jax
import jax.numpy as jnp
from jax import lax

DIN = 8192
DOUT = 8192
KA = 4096
KG = 4096
TOK_DEV = 128
SEQ_DEV = 4
TOKENS = 4096
N_DP = 32


def draw_seq_ids(key, part):
    key = jax.random.fold_in(key, 11)
    shards = TOKENS // TOK_DEV
    keys = jax.random.split(key, shards)

    def one_shard(shard_key, shard):
        order = jax.random.permutation(shard_key, TOK_DEV - 1)
        cuts = order[:SEQ_DEV - 1].astype(jnp.int32) + 1
        position = jnp.arange(TOK_DEV, dtype=jnp.int32)
        segment = jnp.sum((position[:, None] >= cuts[None, :]).astype(jnp.int32), axis=1)
        return shard * SEQ_DEV + segment
    ids = jax.vmap(one_shard)(keys, jnp.arange(shards, dtype=jnp.int32))
    return ids.reshape(TOKENS).astype(jnp.int32)


def levels(key, shape, pieces, least, top_value):
    gain = 1.0
    for dim, shards_of in pieces:
        draws = jax.random.uniform(jax.random.fold_in(jax.random.fold_in(key, 6), dim), (shards_of,), jnp.float32, least / len(pieces), top_value / len(pieces))
        gain = gain * jnp.repeat(jnp.exp(draws), shape[dim] // shards_of).reshape((-1,) + (1,) * (len(shape) - 1 - dim))
    return gain


def bell_draw(key, dims, scale, reach, cuts=(), kind=jnp.bfloat16):
    values = scale * jax.random.normal(key, dims, jnp.float32)
    if cuts:
        values = values * levels(key, dims, cuts, -0.22, 0.18)
    return jnp.clip(values, -reach, reach).astype(kind)


def setup_inputs(seed: int = 0) -> dict:
    key_list = jax.random.split(jax.random.key(seed), 6)
    return {
        "acts": bell_draw(key_list[0], (TOKENS, DIN), 1.0, 6.0, ((0, 32),)),
        "grads": bell_draw(key_list[1], (TOKENS, DOUT), 0.25, 1.5, ((0, 32),)),
        "basis_in": bell_draw(key_list[2], (DIN, KA), DIN ** -0.5, 0.0625, ((0, 32), (1, 16)), jnp.float32),
        "basis_out": bell_draw(key_list[3], (DOUT, KG), DOUT ** -0.5, 0.0625, ((0, 32), (1, 16)), jnp.float32),
        "seq_ids": draw_seq_ids(jax.random.fold_in(key_list[5], 71), 0),
    }


def rotate(values, basis):
    rows = values.shape[1] // N_DP

    def step(total, index):
        start = (index * rows).astype(jnp.int32)
        piece = lax.dynamic_slice_in_dim(values, start, rows, 1).astype(jnp.float32)
        block = lax.dynamic_slice_in_dim(basis, start, rows, 0)
        partial_value = jnp.dot(piece, block, precision=lax.Precision.HIGHEST, preferred_element_type=jnp.float32)
        rounded = lax.optimization_barrier(partial_value.astype(jnp.bfloat16))
        return total + rounded.astype(jnp.float32), None

    start_total = jnp.zeros((values.shape[0], basis.shape[1]), jnp.float32)
    total, _ = lax.scan(step, start_total, jnp.arange(N_DP, dtype=jnp.int32))
    return total.astype(jnp.bfloat16)


def reference(acts, grads, basis_in, basis_out, seq_ids):
    rot_in = rotate(acts, basis_in)
    rot_out = rotate(grads, basis_out)
    slots = seq_ids % SEQ_DEV

    def shard(total, index):
        start = (index * TOK_DEV).astype(jnp.int32)
        right = lax.dynamic_slice_in_dim(rot_in, start, TOK_DEV, 0).astype(jnp.float32)
        left = lax.dynamic_slice_in_dim(rot_out, start, TOK_DEV, 0).astype(jnp.float32)
        local = lax.dynamic_slice_in_dim(slots, start, TOK_DEV, 0)
        member = (local[None, :] == jnp.arange(SEQ_DEV, dtype=jnp.int32)[:, None]).astype(jnp.float32)
        masked = member[:, :, None] * left[None, :, :]
        per_seq = jnp.einsum("sti,tj->sij", masked, right, precision=lax.Precision.HIGHEST)
        return total + jnp.sum(per_seq * per_seq, axis=0), None

    start_total = jnp.zeros((KG, KA), jnp.float32)
    total, _ = lax.scan(shard, start_total, jnp.arange(N_DP, dtype=jnp.int32))
    return total / jnp.float32(SEQ_DEV * N_DP)
```

```python
import jax
import jax.numpy as jnp
from jax import lax
from jax.experimental import pallas as pl
from jax.experimental.pallas import tpu as pltpu
from jax.sharding import PartitionSpec as P

SEQ_DEV = 4
TOK = 128
NZ = 16
NH = 2
COLS = 256
ROWS = 256
HALF = NZ * ROWS
TAG = 16
MESH = pl.DeviceIdType.MESH
F32 = jnp.float32
BF16 = jnp.bfloat16


class Ring:
    hops = ((8, 7), (7, 8))

    def __init__(self, buf, cuts, send, recv, h, z):
        self.buf, self.cuts, self.send, self.recv, self.h, self.z = buf, cuts, send, recv, h, z

    def copy(self, way, part, t, origin):
        sign = 1 if way == 0 else -1
        low, size = self.cuts[part]
        piece = self.buf.at[origin, pl.ds(low, size)]
        return pltpu.make_async_remote_copy(
            src_ref=piece, dst_ref=piece,
            send_sem=self.send.at[way, part, t], recv_sem=self.recv.at[way, part, t],
            device_id={"dp": self.h * NZ + lax.rem(self.z + sign + NZ, NZ)}, device_id_type=MESH)

    def slot(self, way, t):
        sign = 1 if way == 0 else -1
        return lax.rem(self.z - sign * t + NZ, NZ)

    def step(self, s):
        for part in range(2):
            for way in range(2):
                hops = self.hops[way][part]
                if 1 <= s <= hops:
                    self.copy(way, part, s - 1, self.slot(way, s)).wait_recv()
                if s < hops:
                    self.copy(way, part, s, self.slot(way, s)).start()

    def slots(self, s):
        if s == 0:
            return [self.z]
        if s == NZ // 2:
            return [self.slot(0, s)]
        return [self.slot(0, s), self.slot(1, s)]

    def finish(self):
        for part in range(2):
            for way in range(2):
                for t in range(self.hops[way][part]):
                    self.copy(way, part, t, self.slot(way, t)).wait_send()


def kernel(acts, grads, basis_in, basis_out, seq, out,
           a_in, a_out, b_in, b_out, f_in, f_out, acc, psend, precv, rots, gath, right, osum, orecv,
           load, in_s, in_r, out_s, out_r, g_s, g_r, y_s, y_r, k_s, k_r, h_s, h_r, p_s, p_r, q_s, q_r, t_s, t_r):
    blk, pair, dp = lax.axis_index("blk"), lax.axis_index("pair"), lax.axis_index("dp")
    x, core = blk // 2, lax.rem(blk, 2)
    h, z = dp // NZ, lax.rem(dp, NZ)
    c = blk * 2 + pair
    zc = lax.rem(lax.rem(c, 8) + 7, 8) * 2 + c // 8
    cz = lax.rem(z // 2 + 1, 8) + 8 * lax.rem(z, 2)
    row0 = pl.multiple_of(core * 64, 64)
    other0 = pl.multiple_of((1 - core) * 64, 64)

    across = {"pair": 1 - pair, "dp": (1 - h) * NZ + z}
    twin = {"dp": (1 - h) * NZ + z}
    sibling = {"blk": x * 2 + 1 - core}
    peers = [(dx, dy) for dx in range(4) for dy in range(2) if (dx, dy) != (0, 0)]

    def peer(dx, dy):
        return {"blk": lax.rem(x + dx, 4) * 2 + core, "pair": lax.rem(pair + dy, 2)}

    def collected(dx, dy, k):
        of = (lax.rem(x - dx + 4, 4) * 2 + k) * 2 + lax.rem(pair + dy, 2)
        return lax.rem(lax.rem(of, 8) + 7, 8) * 2 + of // 8

    mine = pl.ds(pl.multiple_of(h * HALF, HALF), HALF)
    theirs = pl.ds(pl.multiple_of((1 - h) * HALF, HALF), HALF)
    loads = [
        pltpu.make_async_copy(basis_in, f_in, load.at[0]),
        pltpu.make_async_copy(basis_out, f_out, load.at[1]),
        pltpu.make_async_copy(acts.at[:, mine], a_in.at[pl.ds(0, TOK)], load.at[2]),
        pltpu.make_async_copy(grads.at[:, mine], a_out.at[pl.ds(0, TOK)], load.at[3]),
    ]
    for one in loads:
        one.start()

    barrier = pltpu.get_barrier_semaphore()
    greet = [
        {"dp": h * NZ + lax.rem(z + 1, NZ)},
        {"dp": h * NZ + lax.rem(z + NZ - 1, NZ)},
        across, twin, sibling,
        {"blk": (z // 2) // 2, "pair": lax.rem(z // 2, 2), "dp": h * NZ + zc},
        {"blk": (z // 2) // 2 + 4, "pair": lax.rem(z // 2, 2), "dp": h * NZ + zc},
    ] + [peer(dx, dy) for dx, dy in peers]
    for device in greet:
        pl.semaphore_signal(barrier, inc=1, device_id=device, device_id_type=MESH)

    loads[0].wait()
    b_in[z] = f_in[...].astype(BF16)
    loads[1].wait()
    b_out[z] = f_out[...].astype(BF16)
    tags = jnp.bitwise_and(seq[...], SEQ_DEV - 1).astype(F32)
    gath[z, COLS:COLS + TAG] = jnp.broadcast_to(tags, (TAG, TOK)).astype(BF16)
    osum[...] = jnp.zeros_like(osum)
    acc[...] = jnp.zeros_like(acc)

    pl.semaphore_wait(barrier, len(greet))

    halves = ((0, ROWS // 2), (ROWS // 2, ROWS // 2))
    ring_in = Ring(b_in, halves, in_s, in_r, h, z)
    ring_out = Ring(b_out, halves, out_s, out_r, h, z)
    ring_g = Ring(gath, ((0, 144), (144, 128)), g_s, g_r, h, z)

    def y_copy(i):
        source, held = ((acts, a_in), (grads, a_out))[i]
        return pltpu.make_async_remote_copy(
            src_ref=source.at[pl.ds(row0, 64), theirs], dst_ref=held.at[pl.ds(TOK + row0, 64)],
            send_sem=y_s.at[i], recv_sem=y_r.at[i], device_id=across, device_id_type=MESH)

    def k_copy(i, first):
        piece = (a_in, a_out)[i].at[pl.ds(TOK + first, 64)]
        return pltpu.make_async_remote_copy(
            src_ref=piece, dst_ref=piece, send_sem=k_s.at[i], recv_sem=k_r.at[i],
            device_id=sibling, device_id_type=MESH)

    def h_copy(i):
        return pltpu.make_async_remote_copy(
            src_ref=psend.at[i], dst_ref=precv.at[i], send_sem=h_s.at[i], recv_sem=h_r.at[i],
            device_id=twin, device_id_type=MESH)

    def p_copy(q):
        return pltpu.make_async_remote_copy(
            src_ref=rots.at[q], dst_ref=right.at[z, c // 8], send_sem=p_s.at[q], recv_sem=p_r.at[c // 8],
            device_id={"blk": cz // 2, "pair": lax.rem(cz, 2), "dp": h * NZ + 2 * lax.rem(c, 8) + q},
            device_id_type=MESH)

    def p_arrive(j):
        piece = right.at[zc, j]
        pltpu.make_async_remote_copy(
            src_ref=piece, dst_ref=piece, send_sem=p_s.at[0], recv_sem=p_r.at[j],
            device_id=twin, device_id_type=MESH).wait_recv()

    def q_copy(n, block):
        piece = right.at[block]
        return pltpu.make_async_remote_copy(
            src_ref=piece, dst_ref=piece, send_sem=q_s.at[n], recv_sem=q_r.at[n],
            device_id=peer(*peers[n]), device_id_type=MESH)

    def t_copy(n, block):
        piece = right.at[block]
        return pltpu.make_async_remote_copy(
            src_ref=piece, dst_ref=piece, send_sem=t_s.at[n], recv_sem=t_r.at[n],
            device_id=sibling, device_id_type=MESH)

    def add_block(i, slot):
        held, basis = ((a_in, b_in), (a_out, b_out))[i]
        columns = pl.ds(pl.multiple_of(slot * ROWS, ROWS), ROWS)
        acc[i] += jnp.dot(held[:, columns], basis[slot], preferred_element_type=F32)

    def square(slot):
        left = gath[slot, 0:COLS]
        ids = gath[slot, COLS:COLS + TAG].astype(F32)[0:1]
        block = jnp.concatenate([right[slot, 0], right[slot, 1]], axis=1)
        total = None
        for s in range(SEQ_DEV):
            member = jnp.where(ids == F32(s), F32(1), F32(0)).astype(BF16)
            product = jnp.dot(left * member, block, preferred_element_type=F32)
            product = product * product
            total = product if total is None else total + product
        osum[0] += total[:, :TOK]
        osum[1] += total[:, TOK:]

    ring_in.step(0)
    y_copy(0).start()
    for s in range(1, 9):
        if s == 8:
            ring_out.step(0)
        ring_in.step(s)
        if s == 5:
            y_copy(0).wait_recv()
            k_copy(0, row0).start()
            y_copy(1).start()
    loads[2].wait()
    k_copy(0, other0).wait_recv()
    ring_out.step(1)

    @pl.loop(0, NZ)
    def _(slot):
        add_block(0, slot)

    psend[0] = acc[0, TOK:].astype(BF16)
    h_copy(0).start()

    for s in range(2, 9):
        ring_out.step(s)
        if s == 2:
            h_copy(0).wait_recv()
            rotated = (acc[0, :TOK] + precv[0].astype(F32)).astype(BF16)
            rots[0] = rotated[:, :TOK]
            rots[1] = rotated[:, TOK:]
            for q in range(2):
                p_copy(q).start()
            y_copy(1).wait_recv()
            k_copy(1, row0).start()
        if s == 3:
            for j in range(2):
                p_arrive(j)
            for n in range(len(peers)):
                q_copy(n, zc).start()
            t_copy(7, zc).start()
        if s == 4:
            loads[3].wait()
            k_copy(1, other0).wait_recv()

            @pl.loop(0, 2 * s + 1)
            def _(i):
                add_block(1, lax.rem(z + NZ - 4 + i, NZ))
        if s > 4:
            for slot in ring_out.slots(s):
                add_block(1, slot)
        if s == 6:
            for n, (dx, dy) in enumerate(peers):
                block = collected(dx, dy, core)
                q_copy(n, block).wait_recv()
                t_copy(n, block).start()

    psend[1] = acc[1, TOK:].astype(BF16)
    h_copy(1).start()
    for n, (dx, dy) in enumerate(peers):
        t_copy(n, collected(dx, dy, 1 - core)).wait_recv()
    t_copy(7, collected(0, 0, 1 - core)).wait_recv()
    h_copy(1).wait_recv()
    rotated = acc[1, :TOK] + precv[1].astype(F32)
    gath[z, 0:COLS] = rotated.T.astype(BF16)

    for s in range(9):
        ring_g.step(s)
        for slot in ring_g.slots(s):
            square(slot)

    last = pltpu.make_async_remote_copy(
        src_ref=osum.at[1 - h], dst_ref=orecv, send_sem=h_s.at[2], recv_sem=h_r.at[2],
        device_id=twin, device_id_type=MESH)
    last.start()

    ring_in.finish()
    ring_out.finish()
    ring_g.finish()
    for i in range(2):
        y_copy(i).wait_send()
        k_copy(i, row0).wait_send()
        h_copy(i).wait_send()
        p_copy(i).wait_send()
    for n, (dx, dy) in enumerate(peers):
        q_copy(n, zc).wait_send()
        t_copy(n, collected(dx, dy, core)).wait_send()
    t_copy(7, zc).wait_send()

    last.wait_recv()
    out[...] = (osum[h] + orecv[...]) * F32(1.0 / (SEQ_DEV * NZ * NH))
    last.wait_send()


def on_device(acts, grads, basis_in, basis_out, seq_ids):
    dma = pltpu.SemaphoreType.DMA
    ring = dma((2, 2, 8))
    return pl.pallas_call(
        kernel,
        out_shape=jax.ShapeDtypeStruct((COLS, TOK), F32),
        in_specs=[pl.BlockSpec(memory_space=pl.ANY)] * 4 + [pl.BlockSpec(memory_space=pltpu.VMEM)],
        out_specs=pl.BlockSpec(memory_space=pltpu.VMEM),
        scratch_shapes=[
            pltpu.VMEM((NH * TOK, HALF), BF16),
            pltpu.VMEM((NH * TOK, HALF), BF16),
            pltpu.VMEM((NZ, ROWS, COLS), BF16),
            pltpu.VMEM((NZ, ROWS, COLS), BF16),
            pltpu.VMEM((ROWS, COLS), F32),
            pltpu.VMEM((ROWS, COLS), F32),
            pltpu.VMEM((2, NH * TOK, COLS), F32),
            pltpu.VMEM((2, TOK, COLS), BF16),
            pltpu.VMEM((2, TOK, COLS), BF16),
            pltpu.VMEM((2, TOK, TOK), BF16),
            pltpu.VMEM((NZ, COLS + TAG, TOK), BF16),
            pltpu.VMEM((NZ, NH, TOK, TOK), BF16),
            pltpu.VMEM((NH, COLS, TOK), F32),
            pltpu.VMEM((COLS, TOK), F32),
            dma((4,)),
            ring, ring, ring, ring, ring, ring,
            dma((2,)), dma((2,)), dma((2,)), dma((2,)), dma((3,)), dma((3,)),
            dma((2,)), dma((2,)), dma((7,)), dma((7,)), dma((8,)), dma((8,)),
        ],
        compiler_params=pltpu.CompilerParams(
            collective_id=0, has_side_effects=True, vmem_limit_bytes=40 * 1024 * 1024),
        cost_estimate=pl.CostEstimate(flops=3_300_000_000, bytes_accessed=8_000_000, transcendentals=0),
    )(acts, grads, basis_in, basis_out, seq_ids.reshape(1, TOK))


def solution(mesh):
    return jax.shard_map(
        on_device,
        mesh=mesh,
        in_specs=(
            P("dp", None),
            P("dp", None),
            P("dp", ("blk", "pair")),
            P("dp", ("blk", "pair")),
            P("dp"),
        ),
        out_specs=P(("blk", "pair"), "dp"),
        check_vma=False,
    )
```

```python
import jax
import jax.numpy as jnp
from jax import lax
from jax.experimental import pallas as pl
from jax.experimental.pallas import tpu as pltpu
from jax.sharding import PartitionSpec as P

SEQ_DEV = 4
TOK = 128
NZ = 16
NH = 2
COLS = 256
ROWS = 256
HALF = NZ * ROWS
LAG = 4
TAG = 16
MESH = pl.DeviceIdType.MESH
F32 = jnp.float32
BF16 = jnp.bfloat16


class Ring:
    hops = ((8, 7), (7, 8))

    def __init__(self, buf, cuts, send, recv, h, z):
        self.buf, self.cuts, self.send, self.recv, self.h, self.z = buf, cuts, send, recv, h, z

    def copy(self, way, part, t, origin):
        sign = 1 if way == 0 else -1
        low, size = self.cuts[part]
        piece = self.buf.at[origin, pl.ds(low, size)]
        return pltpu.make_async_remote_copy(
            src_ref=piece, dst_ref=piece,
            send_sem=self.send.at[way, part, t], recv_sem=self.recv.at[way, part, t],
            device_id={"dp": self.h * NZ + lax.rem(self.z + sign + NZ, NZ)}, device_id_type=MESH)

    def slot(self, way, t):
        sign = 1 if way == 0 else -1
        return lax.rem(self.z - sign * t + NZ, NZ)

    def step(self, s):
        for part in range(2):
            for way in range(2):
                hops = self.hops[way][part]
                if 1 <= s <= hops:
                    self.copy(way, part, s - 1, self.slot(way, s)).wait_recv()
                if s < hops:
                    self.copy(way, part, s, self.slot(way, s)).start()

    def slots(self, s):
        if s == 0:
            return [self.z]
        if s == NZ // 2:
            return [self.slot(0, s)]
        return [self.slot(0, s), self.slot(1, s)]

    def finish(self):
        for part in range(2):
            for way in range(2):
                for t in range(self.hops[way][part]):
                    self.copy(way, part, t, self.slot(way, t)).wait_send()


def kernel(acts, grads, basis_in, basis_out, seq, out,
           a_in, a_out, b_in, b_out, f_in, f_out, acc, psend, precv, rots, gath, right, osum, orecv,
           load, in_s, in_r, out_s, out_r, g_s, g_r, y_s, y_r, k_s, k_r, h_s, h_r, p_s, p_r, q_s, q_r, t_s, t_r):
    blk, pair, dp = lax.axis_index("blk"), lax.axis_index("pair"), lax.axis_index("dp")
    x, core = blk // 2, lax.rem(blk, 2)
    h, z = dp // NZ, lax.rem(dp, NZ)
    c = blk * 2 + pair
    zc = lax.rem(lax.rem(c, 8) + 7, 8) * 2 + c // 8
    cz = lax.rem(z // 2 + 1, 8) + 8 * lax.rem(z, 2)
    row0 = pl.multiple_of(core * 64, 64)
    other0 = pl.multiple_of((1 - core) * 64, 64)

    across = {"pair": 1 - pair, "dp": (1 - h) * NZ + z}
    twin = {"dp": (1 - h) * NZ + z}
    sibling = {"blk": x * 2 + 1 - core}
    peers = [(dx, dy) for dx in range(4) for dy in range(2) if (dx, dy) != (0, 0)]

    def peer(dx, dy):
        return {"blk": lax.rem(x + dx, 4) * 2 + core, "pair": lax.rem(pair + dy, 2)}

    def collected(dx, dy, k):
        of = (lax.rem(x - dx + 4, 4) * 2 + k) * 2 + lax.rem(pair + dy, 2)
        return lax.rem(lax.rem(of, 8) + 7, 8) * 2 + of // 8

    mine = pl.ds(pl.multiple_of(h * HALF, HALF), HALF)
    theirs = pl.ds(pl.multiple_of((1 - h) * HALF, HALF), HALF)
    loads = [
        pltpu.make_async_copy(basis_in, f_in, load.at[0]),
        pltpu.make_async_copy(basis_out, f_out, load.at[1]),
        pltpu.make_async_copy(acts.at[:, mine], a_in.at[pl.ds(0, TOK)], load.at[2]),
        pltpu.make_async_copy(grads.at[:, mine], a_out.at[pl.ds(0, TOK)], load.at[3]),
    ]
    for one in loads:
        one.start()

    barrier = pltpu.get_barrier_semaphore()
    greet = [
        {"dp": h * NZ + lax.rem(z + 1, NZ)},
        {"dp": h * NZ + lax.rem(z + NZ - 1, NZ)},
        across, twin, sibling,
        {"blk": (z // 2) // 2, "pair": lax.rem(z // 2, 2), "dp": h * NZ + zc},
        {"blk": (z // 2) // 2 + 4, "pair": lax.rem(z // 2, 2), "dp": h * NZ + zc},
    ] + [peer(dx, dy) for dx, dy in peers]
    for device in greet:
        pl.semaphore_signal(barrier, inc=1, device_id=device, device_id_type=MESH)

    loads[0].wait()
    b_in[z] = f_in[...].astype(BF16)
    loads[1].wait()
    b_out[z] = f_out[...].astype(BF16)
    tags = jnp.bitwise_and(seq[...], SEQ_DEV - 1).astype(F32)
    gath[z, COLS:COLS + TAG] = jnp.broadcast_to(tags, (TAG, TOK)).astype(BF16)
    osum[...] = jnp.zeros_like(osum)
    acc[...] = jnp.zeros_like(acc)

    pl.semaphore_wait(barrier, len(greet))

    halves = ((0, ROWS // 2), (ROWS // 2, ROWS // 2))
    ring_in = Ring(b_in, halves, in_s, in_r, h, z)
    ring_out = Ring(b_out, halves, out_s, out_r, h, z)
    ring_g = Ring(gath, ((0, 144), (144, 128)), g_s, g_r, h, z)

    def y_copy(i):
        source, held = ((acts, a_in), (grads, a_out))[i]
        return pltpu.make_async_remote_copy(
            src_ref=source.at[pl.ds(row0, 64), theirs], dst_ref=held.at[pl.ds(TOK + row0, 64)],
            send_sem=y_s.at[i], recv_sem=y_r.at[i], device_id=across, device_id_type=MESH)

    def k_copy(i, first):
        piece = (a_in, a_out)[i].at[pl.ds(TOK + first, 64)]
        return pltpu.make_async_remote_copy(
            src_ref=piece, dst_ref=piece, send_sem=k_s.at[i], recv_sem=k_r.at[i],
            device_id=sibling, device_id_type=MESH)

    def h_copy(i):
        return pltpu.make_async_remote_copy(
            src_ref=psend.at[i], dst_ref=precv.at[i], send_sem=h_s.at[i], recv_sem=h_r.at[i],
            device_id=twin, device_id_type=MESH)

    def p_copy(q):
        return pltpu.make_async_remote_copy(
            src_ref=rots.at[q], dst_ref=right.at[z, c // 8], send_sem=p_s.at[q], recv_sem=p_r.at[c // 8],
            device_id={"blk": cz // 2, "pair": lax.rem(cz, 2), "dp": h * NZ + 2 * lax.rem(c, 8) + q},
            device_id_type=MESH)

    def p_arrive(j):
        piece = right.at[zc, j]
        pltpu.make_async_remote_copy(
            src_ref=piece, dst_ref=piece, send_sem=p_s.at[0], recv_sem=p_r.at[j],
            device_id=twin, device_id_type=MESH).wait_recv()

    def q_copy(n, block):
        piece = right.at[block]
        return pltpu.make_async_remote_copy(
            src_ref=piece, dst_ref=piece, send_sem=q_s.at[n], recv_sem=q_r.at[n],
            device_id=peer(*peers[n]), device_id_type=MESH)

    def t_copy(n, block):
        piece = right.at[block]
        return pltpu.make_async_remote_copy(
            src_ref=piece, dst_ref=piece, send_sem=t_s.at[n], recv_sem=t_r.at[n],
            device_id=sibling, device_id_type=MESH)

    def add_block(i, slot):
        held, basis = ((a_in, b_in), (a_out, b_out))[i]
        columns = pl.ds(pl.multiple_of(slot * ROWS, ROWS), ROWS)
        acc[i] += jnp.dot(held[:, columns], basis[slot], preferred_element_type=F32)

    def square(slot):
        left = gath[slot, 0:COLS]
        ids = gath[slot, COLS:COLS + TAG].astype(F32)[0:1]
        block = jnp.concatenate([right[slot, 0], right[slot, 1]], axis=1)
        total = None
        for s in range(SEQ_DEV):
            member = jnp.where(ids == F32(s), F32(1), F32(0)).astype(BF16)
            product = jnp.dot(left * member, block, preferred_element_type=F32)
            product = product * product
            total = product if total is None else total + product
        osum[0] += total[:, :TOK]
        osum[1] += total[:, TOK:]

    def add_blocks(i, near, far):
        @pl.loop(2 * near, 2 * far + 2)
        def _(n):
            add_block(i, lax.rem(z + NZ + (2 * lax.rem(n, 2) - 1) * (n // 2), NZ))

    for m in range(LAG + 9):
        if m <= 8:
            ring_in.step(m)
        if m >= LAG:
            ring_out.step(m - LAG)
        if m == 0:
            y_copy(0).start()
        if m == 4:
            y_copy(0).wait_recv()
            k_copy(0, row0).start()
            y_copy(1).start()
        if m == 5:
            loads[2].wait()
            k_copy(0, other0).wait_recv()
            add_block(0, z)
            add_blocks(0, 1, 2)
        if m == 6:
            add_blocks(0, 3, 4)
        if m == 7:
            add_blocks(0, 5, 7)
            y_copy(1).wait_recv()
            k_copy(1, row0).start()
        if m == 8:
            add_block(0, ring_in.slots(8)[0])
            psend[0] = acc[0, TOK:].astype(BF16)
            h_copy(0).start()
        if m == 9:
            h_copy(0).wait_recv()
            rotated = (acc[0, :TOK] + precv[0].astype(F32)).astype(BF16)
            rots[0] = rotated[:, :TOK]
            rots[1] = rotated[:, TOK:]
            for q in range(2):
                p_copy(q).start()
            loads[3].wait()
            k_copy(1, other0).wait_recv()
            add_block(1, z)
            add_blocks(1, 1, 2)
        if m == 10:
            for j in range(2):
                p_arrive(j)
            for n in range(len(peers)):
                q_copy(n, zc).start()
            t_copy(7, zc).start()
            add_blocks(1, 3, 5)
        if m == 11:
            for n, (dx, dy) in enumerate(peers):
                block = collected(dx, dy, core)
                q_copy(n, block).wait_recv()
                t_copy(n, block).start()
            add_blocks(1, 6, 7)
        if m == 12:
            add_block(1, ring_out.slots(8)[0])

    psend[1] = acc[1, TOK:].astype(BF16)
    h_copy(1).start()
    for n, (dx, dy) in enumerate(peers):
        t_copy(n, collected(dx, dy, 1 - core)).wait_recv()
    t_copy(7, collected(0, 0, 1 - core)).wait_recv()
    h_copy(1).wait_recv()
    rotated = acc[1, :TOK] + precv[1].astype(F32)
    gath[z, 0:COLS] = rotated.T.astype(BF16)

    for s in range(9):
        ring_g.step(s)
        for slot in ring_g.slots(s):
            square(slot)

    last = pltpu.make_async_remote_copy(
        src_ref=osum.at[1 - h], dst_ref=orecv, send_sem=h_s.at[2], recv_sem=h_r.at[2],
        device_id=twin, device_id_type=MESH)
    last.start()

    ring_in.finish()
    ring_out.finish()
    ring_g.finish()
    for i in range(2):
        y_copy(i).wait_send()
        k_copy(i, row0).wait_send()
        h_copy(i).wait_send()
        p_copy(i).wait_send()
    for n, (dx, dy) in enumerate(peers):
        q_copy(n, zc).wait_send()
        t_copy(n, collected(dx, dy, core)).wait_send()
    t_copy(7, zc).wait_send()

    last.wait_recv()
    out[...] = (osum[h] + orecv[...]) * F32(1.0 / (SEQ_DEV * NZ * NH))
    last.wait_send()


def on_device(acts, grads, basis_in, basis_out, seq_ids):
    dma = pltpu.SemaphoreType.DMA
    ring = dma((2, 2, 8))
    return pl.pallas_call(
        kernel,
        out_shape=jax.ShapeDtypeStruct((COLS, TOK), F32),
        in_specs=[pl.BlockSpec(memory_space=pl.ANY)] * 4 + [pl.BlockSpec(memory_space=pltpu.VMEM)],
        out_specs=pl.BlockSpec(memory_space=pltpu.VMEM),
        scratch_shapes=[
            pltpu.VMEM((NH * TOK, HALF), BF16),
            pltpu.VMEM((NH * TOK, HALF), BF16),
            pltpu.VMEM((NZ, ROWS, COLS), BF16),
            pltpu.VMEM((NZ, ROWS, COLS), BF16),
            pltpu.VMEM((ROWS, COLS), F32),
            pltpu.VMEM((ROWS, COLS), F32),
            pltpu.VMEM((2, NH * TOK, COLS), F32),
            pltpu.VMEM((2, TOK, COLS), BF16),
            pltpu.VMEM((2, TOK, COLS), BF16),
            pltpu.VMEM((2, TOK, TOK), BF16),
            pltpu.VMEM((NZ, COLS + TAG, TOK), BF16),
            pltpu.VMEM((NZ, NH, TOK, TOK), BF16),
            pltpu.VMEM((NH, COLS, TOK), F32),
            pltpu.VMEM((COLS, TOK), F32),
            dma((4,)),
            ring, ring, ring, ring, ring, ring,
            dma((2,)), dma((2,)), dma((2,)), dma((2,)), dma((3,)), dma((3,)),
            dma((2,)), dma((2,)), dma((7,)), dma((7,)), dma((8,)), dma((8,)),
        ],
        compiler_params=pltpu.CompilerParams(
            collective_id=0, has_side_effects=True, vmem_limit_bytes=62 * 1024 * 1024),
        cost_estimate=pl.CostEstimate(flops=3_300_000_000, bytes_accessed=8_000_000, transcendentals=0),
    )(acts, grads, basis_in, basis_out, seq_ids.reshape(1, TOK))


def solution(mesh):
    return jax.shard_map(
        on_device,
        mesh=mesh,
        in_specs=(
            P("dp", None),
            P("dp", None),
            P("dp", ("blk", "pair")),
            P("dp", ("blk", "pair")),
            P("dp"),
        ),
        out_specs=P(("blk", "pair"), "dp"),
        check_vma=False,
    )
```

```python
import jax
import jax.numpy as jnp
from jax import lax
from jax.experimental import pallas as pl
from jax.experimental.pallas import tpu as pltpu
from jax.sharding import PartitionSpec as P

SEQ_DEV = 4
TOK = 128
NZ = 16
NH = 2
COLS = 256
ROWS = 256
HALF = NZ * ROWS
LAG_A = 2
LAG_B = 5
TAG = 16
MESH = pl.DeviceIdType.MESH
F32 = jnp.float32
BF16 = jnp.bfloat16


class Ring:
    def __init__(self, piece, hops, send, recv, h, z):
        self.piece, self.hops, self.send, self.recv, self.h, self.z = piece, hops, send, recv, h, z

    def slot(self, way, t):
        return lax.rem(self.z + (NZ - t if way == 0 else t), NZ)

    def copy(self, way, part, t, origin):
        piece = self.piece(part, origin)
        return pltpu.make_async_remote_copy(
            src_ref=piece, dst_ref=piece,
            send_sem=self.send.at[way, part, t], recv_sem=self.recv.at[way, part, t],
            device_id={"dp": self.h * NZ + self.slot(1 - way, 1)}, device_id_type=MESH)

    def step(self, s):
        for part in range(len(self.hops)):
            for way in range(2):
                hops = self.hops[part][way]
                if 1 <= s <= hops:
                    self.copy(way, part, s - 1, self.slot(way, s)).wait_recv()
                if s < hops:
                    self.copy(way, part, s, self.slot(way, s)).start()

    def finish(self):
        for part in range(len(self.hops)):
            for way in range(2):
                for t in range(self.hops[part][way]):
                    self.copy(way, part, t, self.slot(way, t)).wait_send()


class Skip:
    def __init__(self, piece, hops, send, recv, h, z):
        self.piece, self.hops, self.send, self.recv, self.h, self.z = piece, hops, send, recv, h, z

    def slot(self, way, t):
        return lax.rem(self.z + (NZ - t if way == 0 else t), NZ)

    def copy(self, way, r, far, origin):
        piece = self.piece(origin)
        return pltpu.make_async_remote_copy(
            src_ref=piece, dst_ref=piece,
            send_sem=self.send.at[way, r, far], recv_sem=self.recv.at[way, r, far],
            device_id={"dp": self.h * NZ + self.slot(1 - way, 1 + far)}, device_id_type=MESH)

    def round(self, r):
        for way in range(2):
            if r >= 1 and 2 * r <= self.hops[way]:
                self.copy(way, r - 1, 1, self.slot(way, 2 * r)).wait_recv()
            if r < 4:
                for far in (1, 0):
                    if 2 * r + 1 + far <= self.hops[way]:
                        self.copy(way, r, far, self.slot(way, 2 * r)).start()
        if r >= 1:
            for way in range(2):
                self.copy(way, r - 1, 0, self.slot(way, 2 * r - 1)).wait_recv()

    def slots(self, r):
        if r == 0:
            return [self.z]
        near = [self.slot(0, 2 * r - 1), self.slot(1, 2 * r - 1), self.slot(0, 2 * r)]
        return near if r == 4 else near + [self.slot(1, 2 * r)]

    def finish(self):
        for way in range(2):
            for r in range(4):
                for far in range(2):
                    if 2 * r + 1 + far <= self.hops[way]:
                        self.copy(way, r, far, self.slot(way, 2 * r)).wait_send()


def kernel(acts, grads, basis_in, basis_out, seq, out,
           a_in, a_out, b_in, b_out, f_in, f_out, acc, accs, psend, precv, psends, precvs, rots, gath, gath2, right,
           osum, orecv,
           load, in_s, in_r, out_s, out_r, out2_s, out2_r, g_s, g_r, g2_s, g2_r,
           y_s, y_r, k_s, k_r, h_s, h_r, p_s, p_r, q_s, q_r, t_s, t_r, o_s, o_r):
    blk, pair, dp = lax.axis_index("blk"), lax.axis_index("pair"), lax.axis_index("dp")
    x, core = blk // 2, lax.rem(blk, 2)
    h, z = dp // NZ, lax.rem(dp, NZ)
    c = blk * 2 + pair
    zc = lax.rem(lax.rem(c, 8) + 7, 8) * 2 + c // 8
    cz = lax.rem(z // 2 + 1, 8) + 8 * lax.rem(z, 2)
    row0 = pl.multiple_of(core * 64, 64)
    other0 = pl.multiple_of((1 - core) * 64, 64)

    across = {"pair": 1 - pair, "dp": (1 - h) * NZ + z}
    twin = {"dp": (1 - h) * NZ + z}
    sibling = {"blk": x * 2 + 1 - core}
    peers = [(dx, dy) for dx in range(4) for dy in range(2) if (dx, dy) != (0, 0)]

    def peer(dx, dy):
        return {"blk": lax.rem(x + dx, 4) * 2 + core, "pair": lax.rem(pair + dy, 2)}

    def collected(dx, dy, k):
        of = (lax.rem(x - dx + 4, 4) * 2 + k) * 2 + lax.rem(pair + dy, 2)
        return lax.rem(lax.rem(of, 8) + 7, 8) * 2 + of // 8

    mine = pl.ds(pl.multiple_of(h * HALF, HALF), HALF)
    theirs = pl.ds(pl.multiple_of((1 - h) * HALF, HALF), HALF)
    loads = [
        pltpu.make_async_copy(basis_in, f_in, load.at[0]),
        pltpu.make_async_copy(basis_out, f_out, load.at[1]),
        pltpu.make_async_copy(acts.at[:, mine], a_in.at[pl.ds(0, TOK)], load.at[2]),
        pltpu.make_async_copy(grads.at[:, mine], a_out.at[pl.ds(0, TOK)], load.at[3]),
    ]
    for one in loads:
        one.start()

    barrier = pltpu.get_barrier_semaphore()
    greet = [
        {"dp": h * NZ + lax.rem(z + 1, NZ)},
        {"dp": h * NZ + lax.rem(z + NZ - 1, NZ)},
        {"dp": h * NZ + lax.rem(z + 2, NZ)},
        {"dp": h * NZ + lax.rem(z + NZ - 2, NZ)},
        across, twin, sibling,
        {"blk": (z // 2) // 2, "pair": lax.rem(z // 2, 2), "dp": h * NZ + zc},
        {"blk": (z // 2) // 2 + 4, "pair": lax.rem(z // 2, 2), "dp": h * NZ + zc},
    ] + [peer(dx, dy) for dx, dy in peers]
    for device in greet:
        pl.semaphore_signal(barrier, inc=1, device_id=device, device_id_type=MESH)

    loads[0].wait()
    b_in[z] = f_in[...].astype(BF16)
    loads[1].wait()
    b_out[0, z] = f_out[:, :TOK].astype(BF16)
    b_out[1, z] = f_out[:, TOK:].astype(BF16)
    tags = jnp.bitwise_and(seq[...], SEQ_DEV - 1).astype(F32)
    gath[z, TOK:TOK + TAG] = jnp.broadcast_to(tags, (TAG, TOK)).astype(BF16)
    osum[...] = jnp.zeros_like(osum)
    acc[...] = jnp.zeros_like(acc)
    accs[...] = jnp.zeros_like(accs)

    pl.semaphore_wait(barrier, len(greet))

    part_rows = ROWS // 2
    ring_in = Ring(lambda part, slot: b_in.at[slot, pl.ds(part * part_rows, part_rows)],
                   ((8, 7), (7, 8)), in_s, in_r, h, z)
    ring_a = Ring(lambda part, slot: b_out.at[0, slot], ((8, 7),), out_s, out_r, h, z)
    ring_b = Ring(lambda part, slot: b_out.at[1, slot], ((7, 8),), out2_s, out2_r, h, z)
    ring_ga = Skip(lambda slot: gath.at[slot], (8, 7), g_s, g_r, h, z)
    ring_gb = Skip(lambda slot: gath2.at[slot], (7, 8), g2_s, g2_r, h, z)

    def y_copy(i):
        source, held = ((acts, a_in), (grads, a_out))[i]
        return pltpu.make_async_remote_copy(
            src_ref=source.at[pl.ds(row0, 64), theirs], dst_ref=held.at[pl.ds(TOK + row0, 64)],
            send_sem=y_s.at[i], recv_sem=y_r.at[i], device_id=across, device_id_type=MESH)

    def k_copy(i, first):
        piece = (a_in, a_out)[i].at[pl.ds(TOK + first, 64)]
        return pltpu.make_async_remote_copy(
            src_ref=piece, dst_ref=piece, send_sem=k_s.at[i], recv_sem=k_r.at[i],
            device_id=sibling, device_id_type=MESH)

    def h_copy(i):
        source, target = (psend, precv) if i == 0 else (psends.at[i - 1], precvs.at[i - 1])
        return pltpu.make_async_remote_copy(
            src_ref=source, dst_ref=target, send_sem=h_s.at[i], recv_sem=h_r.at[i],
            device_id=twin, device_id_type=MESH)

    def o_copy(half):
        return pltpu.make_async_remote_copy(
            src_ref=osum.at[half, 1 - h], dst_ref=orecv.at[half], send_sem=o_s.at[half], recv_sem=o_r.at[half],
            device_id=twin, device_id_type=MESH)

    def p_copy(q):
        return pltpu.make_async_remote_copy(
            src_ref=rots.at[q], dst_ref=right.at[z, c // 8], send_sem=p_s.at[q], recv_sem=p_r.at[c // 8],
            device_id={"blk": cz // 2, "pair": lax.rem(cz, 2), "dp": h * NZ + 2 * lax.rem(c, 8) + q},
            device_id_type=MESH)

    def p_arrive(j):
        piece = right.at[zc, j]
        pltpu.make_async_remote_copy(
            src_ref=piece, dst_ref=piece, send_sem=p_s.at[0], recv_sem=p_r.at[j],
            device_id=twin, device_id_type=MESH).wait_recv()

    def q_copy(n, block):
        piece = right.at[block]
        return pltpu.make_async_remote_copy(
            src_ref=piece, dst_ref=piece, send_sem=q_s.at[n], recv_sem=q_r.at[n],
            device_id=peer(*peers[n]), device_id_type=MESH)

    def t_copy(n, block):
        piece = right.at[block]
        return pltpu.make_async_remote_copy(
            src_ref=piece, dst_ref=piece, send_sem=t_s.at[n], recv_sem=t_r.at[n],
            device_id=sibling, device_id_type=MESH)

    def add_in(slot):
        columns = pl.ds(pl.multiple_of(slot * ROWS, ROWS), ROWS)
        acc[...] += jnp.dot(a_in[:, columns], b_in[slot], preferred_element_type=F32)

    def add_out(half, slot):
        columns = pl.ds(pl.multiple_of(slot * ROWS, ROWS), ROWS)
        accs[half] += jnp.dot(a_out[:, columns], b_out[half, slot], preferred_element_type=F32)

    def around(near, far, add):
        @pl.loop(2 * near, 2 * far + 2)
        def _(n):
            add(lax.rem(z + NZ + (2 * lax.rem(n, 2) - 1) * (n // 2), NZ))

    def add_a(slot):
        add_out(0, slot)

    def add_b(slot):
        add_out(1, slot)

    opposite = lax.rem(z + NZ // 2, NZ)

    def square(half, slot):
        left = gath[slot, 0:TOK] if half == 0 else gath2[slot]
        ids = gath[slot, TOK:TOK + TAG].astype(F32)[0:1]
        block = jnp.concatenate([right[slot, 0], right[slot, 1]], axis=1)
        masked = [left * jnp.where(ids == F32(s), F32(1), F32(0)).astype(BF16) for s in range(SEQ_DEV)]
        product = jnp.dot(jnp.concatenate(masked, axis=0), block, preferred_element_type=F32)
        total = None
        for s in range(SEQ_DEV):
            one = product[s * TOK:(s + 1) * TOK]
            total = one * one if total is None else total + one * one
        osum[half, 0] += total[:, :TOK]
        osum[half, 1] += total[:, TOK:]

    def squares(half, r):
        for slot in ring_ga.slots(r):
            square(half, slot)

    def send_partial(half):
        psends[half] = accs[half, TOK:].astype(BF16)
        h_copy(1 + half).start()

    def turned(half):
        h_copy(1 + half).wait_recv()
        return (accs[half, :TOK] + precvs[half].astype(F32)).T.astype(BF16)

    for m in range(LAG_B + 9):
        if m <= 8:
            ring_in.step(m)
        if LAG_A <= m <= LAG_A + 8:
            ring_a.step(m - LAG_A)
        if m >= LAG_B:
            ring_b.step(m - LAG_B)
        if m == 0:
            y_copy(0).start()
            y_copy(1).start()
        if m == 6:
            y_copy(0).wait_recv()
            k_copy(0, row0).start()
        if m == 7:
            loads[2].wait()
            k_copy(0, other0).wait_recv()
            add_in(z)
            around(1, 4, add_in)
            y_copy(1).wait_recv()
            k_copy(1, row0).start()
        if m == 8:
            around(5, 7, add_in)
            add_in(opposite)
            psend[...] = acc[TOK:].astype(BF16)
            h_copy(0).start()
        if m == 9:
            loads[3].wait()
            k_copy(1, other0).wait_recv()
            add_a(z)
            around(1, 6, add_a)
        if m == 10:
            h_copy(0).wait_recv()
            rotated = (acc[:TOK] + precv[...].astype(F32)).astype(BF16)
            rots[0] = rotated[:, :TOK]
            rots[1] = rotated[:, TOK:]
            for q in range(2):
                p_copy(q).start()
            around(7, 7, add_a)
            add_a(opposite)
            send_partial(0)
        if m == 11:
            for j in range(2):
                p_arrive(j)
            for n in range(len(peers)):
                q_copy(n, zc).start()
            t_copy(7, zc).start()
            add_b(z)
            around(1, 5, add_b)
        if m == 12:
            gath[z, 0:TOK] = turned(0)
            ring_ga.round(0)
            for n, (dx, dy) in enumerate(peers):
                block = collected(dx, dy, core)
                q_copy(n, block).wait_recv()
                t_copy(n, block).start()
            around(6, 7, add_b)
        if m == 13:
            add_b(opposite)
            send_partial(1)

    ring_ga.round(1)
    for n, (dx, dy) in enumerate(peers):
        t_copy(n, collected(dx, dy, 1 - core)).wait_recv()
    t_copy(7, collected(0, 0, 1 - core)).wait_recv()
    squares(0, 0)
    squares(0, 1)
    gath2[z] = turned(1)
    ring_gb.round(0)
    ring_ga.round(2)
    squares(1, 0)
    squares(0, 2)
    ring_gb.round(1)
    ring_ga.round(3)
    squares(1, 1)
    squares(0, 3)
    ring_gb.round(2)
    ring_ga.round(4)
    squares(0, 4)
    o_copy(0).start()
    squares(1, 2)
    ring_gb.round(3)
    squares(1, 3)
    ring_gb.round(4)
    squares(1, 4)
    o_copy(1).start()

    for ring in (ring_in, ring_a, ring_b, ring_ga, ring_gb):
        ring.finish()
    for i in range(2):
        y_copy(i).wait_send()
        k_copy(i, row0).wait_send()
        p_copy(i).wait_send()
    for i in range(3):
        h_copy(i).wait_send()
    for n, (dx, dy) in enumerate(peers):
        q_copy(n, zc).wait_send()
        t_copy(n, collected(dx, dy, core)).wait_send()
    t_copy(7, zc).wait_send()

    for half in range(2):
        o_copy(half).wait_recv()
        out[half * TOK:(half + 1) * TOK] = (osum[half, h] + orecv[half]) * F32(1.0 / (SEQ_DEV * NZ * NH))
    for half in range(2):
        o_copy(half).wait_send()


def on_device(acts, grads, basis_in, basis_out, seq_ids):
    dma = pltpu.SemaphoreType.DMA
    ring, half, skip = dma((2, 2, 8)), dma((2, 1, 8)), dma((2, 4, 2))
    return pl.pallas_call(
        kernel,
        out_shape=jax.ShapeDtypeStruct((COLS, TOK), F32),
        in_specs=[pl.BlockSpec(memory_space=pl.ANY)] * 4 + [pl.BlockSpec(memory_space=pltpu.VMEM)],
        out_specs=pl.BlockSpec(memory_space=pltpu.VMEM),
        scratch_shapes=[
            pltpu.VMEM((NH * TOK, HALF), BF16),
            pltpu.VMEM((NH * TOK, HALF), BF16),
            pltpu.VMEM((NZ, ROWS, COLS), BF16),
            pltpu.VMEM((2, NZ, ROWS, TOK), BF16),
            pltpu.VMEM((ROWS, COLS), F32),
            pltpu.VMEM((ROWS, COLS), F32),
            pltpu.VMEM((NH * TOK, COLS), F32),
            pltpu.VMEM((2, NH * TOK, TOK), F32),
            pltpu.VMEM((TOK, COLS), BF16),
            pltpu.VMEM((TOK, COLS), BF16),
            pltpu.VMEM((2, TOK, TOK), BF16),
            pltpu.VMEM((2, TOK, TOK), BF16),
            pltpu.VMEM((2, TOK, TOK), BF16),
            pltpu.VMEM((NZ, TOK + TAG, TOK), BF16),
            pltpu.VMEM((NZ, TOK, TOK), BF16),
            pltpu.VMEM((NZ, NH, TOK, TOK), BF16),
            pltpu.VMEM((2, NH, TOK, TOK), F32),
            pltpu.VMEM((2, TOK, TOK), F32),
            dma((4,)),
            ring, ring, half, half, half, half, skip, skip, skip, skip,
            dma((2,)), dma((2,)), dma((2,)), dma((2,)), dma((3,)), dma((3,)),
            dma((2,)), dma((2,)), dma((7,)), dma((7,)), dma((8,)), dma((8,)), dma((2,)), dma((2,)),
        ],
        compiler_params=pltpu.CompilerParams(
            collective_id=0, has_side_effects=True, vmem_limit_bytes=62 * 1024 * 1024),
        cost_estimate=pl.CostEstimate(flops=3_300_000_000, bytes_accessed=8_000_000, transcendentals=0),
    )(acts, grads, basis_in, basis_out, seq_ids.reshape(1, TOK))


def solution(mesh):
    return jax.shard_map(
        on_device,
        mesh=mesh,
        in_specs=(
            P("dp", None),
            P("dp", None),
            P("dp", ("blk", "pair")),
            P("dp", ("blk", "pair")),
            P("dp"),
        ),
        out_specs=P(("blk", "pair"), "dp"),
        check_vma=False,
    )
```

```python
import jax
import jax.numpy as jnp
from jax import lax
from jax.experimental import pallas as pl
from jax.experimental.pallas import tpu as pltpu
from jax.sharding import PartitionSpec as P

SEQ_DEV = 4
TOK = 128
NZ = 16
NH = 2
COLS = 256
ROWS = 256
HALF = NZ * ROWS
LAG_IN = 2
LAG_B = 7
TAG = 16
MESH = pl.DeviceIdType.MESH
F32 = jnp.float32
BF16 = jnp.bfloat16


class Ring:
    def __init__(self, piece, hops, send, recv, h, z):
        self.piece, self.hops, self.send, self.recv, self.h, self.z = piece, hops, send, recv, h, z

    def slot(self, way, t):
        return lax.rem(self.z + (NZ - t if way == 0 else t), NZ)

    def copy(self, way, part, t, origin):
        piece = self.piece(part, origin)
        return pltpu.make_async_remote_copy(
            src_ref=piece, dst_ref=piece,
            send_sem=self.send.at[way, part, t], recv_sem=self.recv.at[way, part, t],
            device_id={"dp": self.h * NZ + self.slot(1 - way, 1)}, device_id_type=MESH)

    def step(self, s):
        for part in range(len(self.hops)):
            for way in range(2):
                hops = self.hops[part][way]
                if 1 <= s <= hops:
                    self.copy(way, part, s - 1, self.slot(way, s)).wait_recv()
                if s < hops:
                    self.copy(way, part, s, self.slot(way, s)).start()

    def finish(self):
        for part in range(len(self.hops)):
            for way in range(2):
                for t in range(self.hops[part][way]):
                    self.copy(way, part, t, self.slot(way, t)).wait_send()


class Skip:
    def __init__(self, piece, hops, send, recv, h, z):
        self.piece, self.hops, self.send, self.recv, self.h, self.z = piece, hops, send, recv, h, z

    def slot(self, way, t):
        return lax.rem(self.z + (NZ - t if way == 0 else t), NZ)

    def copy(self, way, r, far, origin):
        piece = self.piece(origin)
        return pltpu.make_async_remote_copy(
            src_ref=piece, dst_ref=piece,
            send_sem=self.send.at[way, r, far], recv_sem=self.recv.at[way, r, far],
            device_id={"dp": self.h * NZ + self.slot(1 - way, 1 + far)}, device_id_type=MESH)

    def round(self, r):
        for way in range(2):
            if r >= 1 and 2 * r <= self.hops[way]:
                self.copy(way, r - 1, 1, self.slot(way, 2 * r)).wait_recv()
            if r < 4:
                for far in (1, 0):
                    if 2 * r + 1 + far <= self.hops[way]:
                        self.copy(way, r, far, self.slot(way, 2 * r)).start()
        if r >= 1:
            for way in range(2):
                self.copy(way, r - 1, 0, self.slot(way, 2 * r - 1)).wait_recv()

    def slots(self, r):
        if r == 0:
            return [self.z]
        near = [self.slot(0, 2 * r - 1), self.slot(1, 2 * r - 1), self.slot(0, 2 * r)]
        return near if r == 4 else near + [self.slot(1, 2 * r)]

    def finish(self):
        for way in range(2):
            for r in range(4):
                for far in range(2):
                    if 2 * r + 1 + far <= self.hops[way]:
                        self.copy(way, r, far, self.slot(way, 2 * r)).wait_send()


def kernel(acts, grads, basis_in, basis_out, seq, out,
           a_in, a_out, b_in, b_out, f_in, f_out, acc, accs, psend, precv, psends, precvs, rots, gath, gath2, right,
           osum, orecv,
           load, in_s, in_r, out_s, out_r, out2_s, out2_r, g_s, g_r, g2_s, g2_r,
           y_s, y_r, k_s, k_r, h_s, h_r, p_s, p_r, q_s, q_r, t_s, t_r, o_s, o_r):
    blk, pair, dp = lax.axis_index("blk"), lax.axis_index("pair"), lax.axis_index("dp")
    x, core = blk // 2, lax.rem(blk, 2)
    h, z = dp // NZ, lax.rem(dp, NZ)
    c = blk * 2 + pair
    zc = lax.rem(lax.rem(c, 8) + 7, 8) * 2 + c // 8
    cz = lax.rem(z // 2 + 1, 8) + 8 * lax.rem(z, 2)
    row0 = pl.multiple_of(core * 64, 64)
    other0 = pl.multiple_of((1 - core) * 64, 64)

    across = {"pair": 1 - pair, "dp": (1 - h) * NZ + z}
    twin = {"dp": (1 - h) * NZ + z}
    sibling = {"blk": x * 2 + 1 - core}
    peers = [(dx, dy) for dx in range(4) for dy in range(2) if (dx, dy) != (0, 0)]

    def peer(dx, dy):
        return {"blk": lax.rem(x + dx, 4) * 2 + core, "pair": lax.rem(pair + dy, 2)}

    def collected(dx, dy, k):
        of = (lax.rem(x - dx + 4, 4) * 2 + k) * 2 + lax.rem(pair + dy, 2)
        return lax.rem(lax.rem(of, 8) + 7, 8) * 2 + of // 8

    mine = pl.ds(pl.multiple_of(h * HALF, HALF), HALF)
    theirs = pl.ds(pl.multiple_of((1 - h) * HALF, HALF), HALF)
    loads = [
        pltpu.make_async_copy(basis_in, f_in, load.at[0]),
        pltpu.make_async_copy(basis_out, f_out, load.at[1]),
        pltpu.make_async_copy(acts.at[:, mine], a_in.at[pl.ds(0, TOK)], load.at[2]),
        pltpu.make_async_copy(grads.at[:, mine], a_out.at[pl.ds(0, TOK)], load.at[3]),
    ]
    for one in loads:
        one.start()

    barrier = pltpu.get_barrier_semaphore()
    greet = [
        {"dp": h * NZ + lax.rem(z + 1, NZ)},
        {"dp": h * NZ + lax.rem(z + NZ - 1, NZ)},
        {"dp": h * NZ + lax.rem(z + 2, NZ)},
        {"dp": h * NZ + lax.rem(z + NZ - 2, NZ)},
        across, twin, sibling,
        {"blk": (z // 2) // 2, "pair": lax.rem(z // 2, 2), "dp": h * NZ + zc},
        {"blk": (z // 2) // 2 + 4, "pair": lax.rem(z // 2, 2), "dp": h * NZ + zc},
    ] + [peer(dx, dy) for dx, dy in peers]
    for device in greet:
        pl.semaphore_signal(barrier, inc=1, device_id=device, device_id_type=MESH)

    loads[0].wait()
    b_in[z] = f_in[...].astype(BF16)
    loads[1].wait()
    b_out[0, z] = f_out[:, :TOK].astype(BF16)
    b_out[1, z] = f_out[:, TOK:].astype(BF16)
    tags = jnp.bitwise_and(seq[...], SEQ_DEV - 1).astype(F32)
    gath[z, TOK:TOK + TAG] = jnp.broadcast_to(tags, (TAG, TOK)).astype(BF16)
    osum[...] = jnp.zeros_like(osum)
    acc[...] = jnp.zeros_like(acc)
    accs[...] = jnp.zeros_like(accs)

    pl.semaphore_wait(barrier, len(greet))

    part_rows = ROWS // 2
    ring_in = Ring(lambda part, slot: b_in.at[slot, pl.ds(part * part_rows, part_rows)],
                   ((8, 7), (7, 8)), in_s, in_r, h, z)
    ring_a = Ring(lambda part, slot: b_out.at[0, slot], ((8, 7),), out_s, out_r, h, z)
    ring_b = Ring(lambda part, slot: b_out.at[1, slot], ((7, 8),), out2_s, out2_r, h, z)
    ring_ga = Skip(lambda slot: gath.at[slot], (8, 7), g_s, g_r, h, z)
    ring_gb = Skip(lambda slot: gath2.at[slot], (7, 8), g2_s, g2_r, h, z)

    def y_copy(i):
        source, held = ((acts, a_in), (grads, a_out))[i]
        return pltpu.make_async_remote_copy(
            src_ref=source.at[pl.ds(row0, 64), theirs], dst_ref=held.at[pl.ds(TOK + row0, 64)],
            send_sem=y_s.at[i], recv_sem=y_r.at[i], device_id=across, device_id_type=MESH)

    def k_copy(i, first):
        piece = (a_in, a_out)[i].at[pl.ds(TOK + first, 64)]
        return pltpu.make_async_remote_copy(
            src_ref=piece, dst_ref=piece, send_sem=k_s.at[i], recv_sem=k_r.at[i],
            device_id=sibling, device_id_type=MESH)

    def h_copy(i):
        source, target = (psend, precv) if i == 0 else (psends.at[i - 1], precvs.at[i - 1])
        return pltpu.make_async_remote_copy(
            src_ref=source, dst_ref=target, send_sem=h_s.at[i], recv_sem=h_r.at[i],
            device_id=twin, device_id_type=MESH)

    def o_copy(half):
        return pltpu.make_async_remote_copy(
            src_ref=osum.at[half, 1 - h], dst_ref=orecv.at[half], send_sem=o_s.at[half], recv_sem=o_r.at[half],
            device_id=twin, device_id_type=MESH)

    def p_copy(q):
        return pltpu.make_async_remote_copy(
            src_ref=rots.at[q], dst_ref=right.at[z, c // 8], send_sem=p_s.at[q], recv_sem=p_r.at[c // 8],
            device_id={"blk": cz // 2, "pair": lax.rem(cz, 2), "dp": h * NZ + 2 * lax.rem(c, 8) + q},
            device_id_type=MESH)

    def p_arrive(j):
        piece = right.at[zc, j]
        pltpu.make_async_remote_copy(
            src_ref=piece, dst_ref=piece, send_sem=p_s.at[0], recv_sem=p_r.at[j],
            device_id=twin, device_id_type=MESH).wait_recv()

    def q_copy(n, block):
        piece = right.at[block]
        return pltpu.make_async_remote_copy(
            src_ref=piece, dst_ref=piece, send_sem=q_s.at[n], recv_sem=q_r.at[n],
            device_id=peer(*peers[n]), device_id_type=MESH)

    def t_copy(n, block):
        piece = right.at[block]
        return pltpu.make_async_remote_copy(
            src_ref=piece, dst_ref=piece, send_sem=t_s.at[n], recv_sem=t_r.at[n],
            device_id=sibling, device_id_type=MESH)

    def add_in(slot):
        columns = pl.ds(pl.multiple_of(slot * ROWS, ROWS), ROWS)
        acc[...] += jnp.dot(a_in[:, columns], b_in[slot], preferred_element_type=F32)

    def add_out(half, slot):
        columns = pl.ds(pl.multiple_of(slot * ROWS, ROWS), ROWS)
        accs[half] += jnp.dot(a_out[:, columns], b_out[half, slot], preferred_element_type=F32)

    def around(near, far, add):
        @pl.loop(2 * near, 2 * far + 2)
        def _(n):
            add(lax.rem(z + NZ + (2 * lax.rem(n, 2) - 1) * (n // 2), NZ))

    def add_a(slot):
        add_out(0, slot)

    def add_b(slot):
        add_out(1, slot)

    opposite = lax.rem(z + NZ // 2, NZ)

    def square(half, slot):
        left = gath[slot, 0:TOK] if half == 0 else gath2[slot]
        ids = gath[slot, TOK:TOK + TAG].astype(F32)[0:1]
        block = jnp.concatenate([right[slot, 0], right[slot, 1]], axis=1)
        masked = [left * jnp.where(ids == F32(s), F32(1), F32(0)).astype(BF16) for s in range(SEQ_DEV)]
        product = jnp.dot(jnp.concatenate(masked, axis=0), block, preferred_element_type=F32)
        total = None
        for s in range(SEQ_DEV):
            one = product[s * TOK:(s + 1) * TOK]
            total = one * one if total is None else total + one * one
        osum[half, 0] += total[:, :TOK]
        osum[half, 1] += total[:, TOK:]

    def squares(half, r):
        for slot in ring_ga.slots(r):
            square(half, slot)

    def send_partial(half):
        psends[half] = accs[half, TOK:].astype(BF16)
        h_copy(1 + half).start()

    def turned(half):
        h_copy(1 + half).wait_recv()
        return (accs[half, :TOK] + precvs[half].astype(F32)).T.astype(BF16)

    for m in range(LAG_B + 9):
        if m <= 8:
            ring_a.step(m)
        if LAG_IN <= m <= LAG_IN + 8:
            ring_in.step(m - LAG_IN)
        if m >= LAG_B:
            ring_b.step(m - LAG_B)
        if m == 0:
            y_copy(1).start()
            y_copy(0).start()
        if m == 5:
            y_copy(1).wait_recv()
            k_copy(1, row0).start()
        if m == 6:
            loads[3].wait()
            k_copy(1, other0).wait_recv()
            add_a(z)
            around(1, 3, add_a)
        if m == 7:
            y_copy(0).wait_recv()
            k_copy(0, row0).start()
            around(4, 6, add_a)
        if m == 8:
            around(7, 7, add_a)
            add_a(opposite)
            send_partial(0)
            loads[2].wait()
            k_copy(0, other0).wait_recv()
            add_in(z)
            around(1, 2, add_in)
        if m == 9:
            gath[z, 0:TOK] = turned(0)
            ring_ga.round(0)
            around(3, 6, add_in)
        if m == 10:
            around(7, 7, add_in)
            add_in(opposite)
            psend[...] = acc[TOK:].astype(BF16)
            h_copy(0).start()
            ring_ga.round(1)
        if m == 11:
            h_copy(0).wait_recv()
            rotated = (acc[:TOK] + precv[...].astype(F32)).astype(BF16)
            rots[0] = rotated[:, :TOK]
            rots[1] = rotated[:, TOK:]
            for q in range(2):
                p_copy(q).start()
            ring_ga.round(2)
            add_b(z)
            around(1, 3, add_b)
        if m == 12:
            ring_ga.round(3)
            for j in range(2):
                p_arrive(j)
            for n in range(len(peers)):
                q_copy(n, zc).start()
            t_copy(7, zc).start()
            around(4, 5, add_b)
        if m == 13:
            ring_ga.round(4)
            around(6, 6, add_b)
        if m == 14:
            for n, (dx, dy) in enumerate(peers):
                block = collected(dx, dy, core)
                q_copy(n, block).wait_recv()
                t_copy(n, block).start()
            around(7, 7, add_b)
        if m == 15:
            add_b(opposite)
            send_partial(1)

    for n, (dx, dy) in enumerate(peers):
        t_copy(n, collected(dx, dy, 1 - core)).wait_recv()
    t_copy(7, collected(0, 0, 1 - core)).wait_recv()
    squares(0, 0)
    squares(0, 1)
    squares(0, 2)
    gath2[z] = turned(1)
    ring_gb.round(0)
    squares(0, 3)
    squares(0, 4)
    o_copy(0).start()
    squares(1, 0)
    for r in range(1, 5):
        ring_gb.round(r)
        squares(1, r)
    o_copy(1).start()

    for ring in (ring_in, ring_a, ring_b, ring_ga, ring_gb):
        ring.finish()
    for i in range(2):
        y_copy(i).wait_send()
        k_copy(i, row0).wait_send()
        p_copy(i).wait_send()
    for i in range(3):
        h_copy(i).wait_send()
    for n, (dx, dy) in enumerate(peers):
        q_copy(n, zc).wait_send()
        t_copy(n, collected(dx, dy, core)).wait_send()
    t_copy(7, zc).wait_send()

    for half in range(2):
        o_copy(half).wait_recv()
        out[half * TOK:(half + 1) * TOK] = (osum[half, h] + orecv[half]) * F32(1.0 / (SEQ_DEV * NZ * NH))
    for half in range(2):
        o_copy(half).wait_send()


def on_device(acts, grads, basis_in, basis_out, seq_ids):
    dma = pltpu.SemaphoreType.DMA
    ring, half, skip = dma((2, 2, 8)), dma((2, 1, 8)), dma((2, 4, 2))
    return pl.pallas_call(
        kernel,
        out_shape=jax.ShapeDtypeStruct((COLS, TOK), F32),
        in_specs=[pl.BlockSpec(memory_space=pl.ANY)] * 4 + [pl.BlockSpec(memory_space=pltpu.VMEM)],
        out_specs=pl.BlockSpec(memory_space=pltpu.VMEM),
        scratch_shapes=[
            pltpu.VMEM((NH * TOK, HALF), BF16),
            pltpu.VMEM((NH * TOK, HALF), BF16),
            pltpu.VMEM((NZ, ROWS, COLS), BF16),
            pltpu.VMEM((2, NZ, ROWS, TOK), BF16),
            pltpu.VMEM((ROWS, COLS), F32),
            pltpu.VMEM((ROWS, COLS), F32),
            pltpu.VMEM((NH * TOK, COLS), F32),
            pltpu.VMEM((2, NH * TOK, TOK), F32),
            pltpu.VMEM((TOK, COLS), BF16),
            pltpu.VMEM((TOK, COLS), BF16),
            pltpu.VMEM((2, TOK, TOK), BF16),
            pltpu.VMEM((2, TOK, TOK), BF16),
            pltpu.VMEM((2, TOK, TOK), BF16),
            pltpu.VMEM((NZ, TOK + TAG, TOK), BF16),
            pltpu.VMEM((NZ, TOK, TOK), BF16),
            pltpu.VMEM((NZ, NH, TOK, TOK), BF16),
            pltpu.VMEM((2, NH, TOK, TOK), F32),
            pltpu.VMEM((2, TOK, TOK), F32),
            dma((4,)),
            ring, ring, half, half, half, half, skip, skip, skip, skip,
            dma((2,)), dma((2,)), dma((2,)), dma((2,)), dma((3,)), dma((3,)),
            dma((2,)), dma((2,)), dma((7,)), dma((7,)), dma((8,)), dma((8,)), dma((2,)), dma((2,)),
        ],
        compiler_params=pltpu.CompilerParams(
            collective_id=0, has_side_effects=True, vmem_limit_bytes=62 * 1024 * 1024),
        cost_estimate=pl.CostEstimate(flops=3_300_000_000, bytes_accessed=8_000_000, transcendentals=0),
    )(acts, grads, basis_in, basis_out, seq_ids.reshape(1, TOK))


def solution(mesh):
    return jax.shard_map(
        on_device,
        mesh=mesh,
        in_specs=(
            P("dp", None),
            P("dp", None),
            P("dp", ("blk", "pair")),
            P("dp", ("blk", "pair")),
            P("dp"),
        ),
        out_specs=P(("blk", "pair"), "dp"),
        check_vma=False,
    )
```

```python
import jax
import jax.numpy as jnp
from jax import lax
from jax.experimental import pallas as pl
from jax.experimental.pallas import tpu as pltpu
from jax.sharding import PartitionSpec as P

SEQ_DEV = 4
TOK = 128
NZ = 16
NH = 2
COLS = 256
ROWS = 256
HALF = NZ * ROWS
LAG_B = 4
TAG = 16
MESH = pl.DeviceIdType.MESH
F32 = jnp.float32
BF16 = jnp.bfloat16


class Ring:
    def __init__(self, piece, hops, send, recv, h, z):
        self.piece, self.hops, self.send, self.recv, self.h, self.z = piece, hops, send, recv, h, z

    def slot(self, way, t):
        return lax.rem(self.z + (NZ - t if way == 0 else t), NZ)

    def copy(self, way, part, t, origin):
        piece = self.piece(part, origin)
        return pltpu.make_async_remote_copy(
            src_ref=piece, dst_ref=piece,
            send_sem=self.send.at[way, part, t], recv_sem=self.recv.at[way, part, t],
            device_id={"dp": self.h * NZ + self.slot(1 - way, 1)}, device_id_type=MESH)

    def step(self, s):
        for part in range(len(self.hops)):
            for way in range(2):
                hops = self.hops[part][way]
                if 1 <= s <= hops:
                    self.copy(way, part, s - 1, self.slot(way, s)).wait_recv()
                if s < hops:
                    self.copy(way, part, s, self.slot(way, s)).start()

    def finish(self):
        for part in range(len(self.hops)):
            for way in range(2):
                for t in range(self.hops[part][way]):
                    self.copy(way, part, t, self.slot(way, t)).wait_send()


class Skip:
    def __init__(self, piece, hops, send, recv, h, z):
        self.piece, self.hops, self.send, self.recv, self.h, self.z = piece, hops, send, recv, h, z

    def slot(self, way, t):
        return lax.rem(self.z + (NZ - t if way == 0 else t), NZ)

    def copy(self, way, r, far, origin):
        piece = self.piece(origin)
        return pltpu.make_async_remote_copy(
            src_ref=piece, dst_ref=piece,
            send_sem=self.send.at[way, r, far], recv_sem=self.recv.at[way, r, far],
            device_id={"dp": self.h * NZ + self.slot(1 - way, 1 + far)}, device_id_type=MESH)

    def round(self, r):
        for way in range(2):
            if r >= 1 and 2 * r <= self.hops[way]:
                self.copy(way, r - 1, 1, self.slot(way, 2 * r)).wait_recv()
            if r < 4:
                for far in (1, 0):
                    if 2 * r + 1 + far <= self.hops[way]:
                        self.copy(way, r, far, self.slot(way, 2 * r)).start()
        if r >= 1:
            for way in range(2):
                self.copy(way, r - 1, 0, self.slot(way, 2 * r - 1)).wait_recv()

    def slots(self, r):
        if r == 0:
            return [self.z]
        near = [self.slot(0, 2 * r - 1), self.slot(1, 2 * r - 1), self.slot(0, 2 * r)]
        return near if r == 4 else near + [self.slot(1, 2 * r)]

    def finish(self):
        for way in range(2):
            for r in range(4):
                for far in range(2):
                    if 2 * r + 1 + far <= self.hops[way]:
                        self.copy(way, r, far, self.slot(way, 2 * r)).wait_send()


def kernel(acts, grads, basis_in, basis_out, seq, out,
           a_in, a_out, b_in, b_out, f_in, f_out, acc, accs, psend, precv, psends, precvs, rots, gath, gath2, right,
           osum, orecv,
           load, in_s, in_r, out_s, out_r, out2_s, out2_r, g_s, g_r, g2_s, g2_r,
           y_s, y_r, k_s, k_r, h_s, h_r, p_s, p_r, q_s, q_r, t_s, t_r, o_s, o_r):
    blk, pair, dp = lax.axis_index("blk"), lax.axis_index("pair"), lax.axis_index("dp")
    x, core = blk // 2, lax.rem(blk, 2)
    h, z = dp // NZ, lax.rem(dp, NZ)
    c = blk * 2 + pair
    zc = lax.rem(lax.rem(c, 8) + 7, 8) * 2 + c // 8
    cz = lax.rem(z // 2 + 1, 8) + 8 * lax.rem(z, 2)
    row0 = pl.multiple_of(core * 64, 64)
    other0 = pl.multiple_of((1 - core) * 64, 64)

    across = {"pair": 1 - pair, "dp": (1 - h) * NZ + z}
    twin = {"dp": (1 - h) * NZ + z}
    sibling = {"blk": x * 2 + 1 - core}
    peers = [(dx, dy) for dx in range(4) for dy in range(2) if (dx, dy) != (0, 0)]

    def peer(dx, dy):
        return {"blk": lax.rem(x + dx, 4) * 2 + core, "pair": lax.rem(pair + dy, 2)}

    def collected(dx, dy, k):
        of = (lax.rem(x - dx + 4, 4) * 2 + k) * 2 + lax.rem(pair + dy, 2)
        return lax.rem(lax.rem(of, 8) + 7, 8) * 2 + of // 8

    mine = pl.ds(pl.multiple_of(h * HALF, HALF), HALF)
    theirs = pl.ds(pl.multiple_of((1 - h) * HALF, HALF), HALF)
    loads = [
        pltpu.make_async_copy(basis_in, f_in, load.at[0]),
        pltpu.make_async_copy(basis_out, f_out, load.at[1]),
        pltpu.make_async_copy(acts.at[:, mine], a_in.at[pl.ds(0, TOK)], load.at[2]),
        pltpu.make_async_copy(grads.at[:, mine], a_out.at[pl.ds(0, TOK)], load.at[3]),
    ]
    for one in loads:
        one.start()

    barrier = pltpu.get_barrier_semaphore()
    greet = [
        {"dp": h * NZ + lax.rem(z + 1, NZ)},
        {"dp": h * NZ + lax.rem(z + NZ - 1, NZ)},
        {"dp": h * NZ + lax.rem(z + 2, NZ)},
        {"dp": h * NZ + lax.rem(z + NZ - 2, NZ)},
        across, twin, sibling,
        {"blk": (z // 2) // 2, "pair": lax.rem(z // 2, 2), "dp": h * NZ + zc},
        {"blk": (z // 2) // 2 + 4, "pair": lax.rem(z // 2, 2), "dp": h * NZ + zc},
    ] + [peer(dx, dy) for dx, dy in peers]
    for device in greet:
        pl.semaphore_signal(barrier, inc=1, device_id=device, device_id_type=MESH)

    loads[0].wait()
    b_in[z] = f_in[...].astype(BF16)
    loads[1].wait()
    b_out[0, z] = f_out[:, :TOK].astype(BF16)
    b_out[1, z] = f_out[:, TOK:].astype(BF16)
    tags = jnp.bitwise_and(seq[...], SEQ_DEV - 1).astype(F32)
    gath[z, TOK:TOK + TAG] = jnp.broadcast_to(tags, (TAG, TOK)).astype(BF16)
    osum[...] = jnp.zeros_like(osum)

    pl.semaphore_wait(barrier, len(greet))

    part_rows = ROWS // 2
    ring_in = Ring(lambda part, slot: b_in.at[slot, pl.ds(part * part_rows, part_rows)],
                   ((8, 7), (7, 8)), in_s, in_r, h, z)
    ring_a = Ring(lambda part, slot: b_out.at[0, slot], ((8, 7),), out_s, out_r, h, z)
    ring_b = Ring(lambda part, slot: b_out.at[1, slot], ((7, 8),), out2_s, out2_r, h, z)
    ring_ga = Skip(lambda slot: gath.at[slot], (8, 7), g_s, g_r, h, z)
    ring_gb = Skip(lambda slot: gath2.at[slot], (7, 8), g2_s, g2_r, h, z)

    def y_copy(i):
        source, held = ((acts, a_in), (grads, a_out))[i]
        return pltpu.make_async_remote_copy(
            src_ref=source.at[pl.ds(row0, 64), theirs], dst_ref=held.at[pl.ds(TOK + row0, 64)],
            send_sem=y_s.at[i], recv_sem=y_r.at[i], device_id=across, device_id_type=MESH)

    def k_copy(i, first):
        piece = (a_in, a_out)[i].at[pl.ds(TOK + first, 64)]
        return pltpu.make_async_remote_copy(
            src_ref=piece, dst_ref=piece, send_sem=k_s.at[i], recv_sem=k_r.at[i],
            device_id=sibling, device_id_type=MESH)

    def h_copy(i):
        source, target = (psend, precv) if i == 0 else (psends.at[i - 1], precvs.at[i - 1])
        return pltpu.make_async_remote_copy(
            src_ref=source, dst_ref=target, send_sem=h_s.at[i], recv_sem=h_r.at[i],
            device_id=twin, device_id_type=MESH)

    def o_copy(half):
        return pltpu.make_async_remote_copy(
            src_ref=osum.at[half, 1 - h], dst_ref=orecv.at[half], send_sem=o_s.at[half], recv_sem=o_r.at[half],
            device_id=twin, device_id_type=MESH)

    def p_copy(q):
        return pltpu.make_async_remote_copy(
            src_ref=rots.at[q], dst_ref=right.at[z, c // 8], send_sem=p_s.at[q], recv_sem=p_r.at[c // 8],
            device_id={"blk": cz // 2, "pair": lax.rem(cz, 2), "dp": h * NZ + 2 * lax.rem(c, 8) + q},
            device_id_type=MESH)

    def p_arrive(j):
        piece = right.at[zc, j]
        pltpu.make_async_remote_copy(
            src_ref=piece, dst_ref=piece, send_sem=p_s.at[0], recv_sem=p_r.at[j],
            device_id=twin, device_id_type=MESH).wait_recv()

    def q_copy(n, block):
        piece = right.at[block]
        return pltpu.make_async_remote_copy(
            src_ref=piece, dst_ref=piece, send_sem=q_s.at[n], recv_sem=q_r.at[n],
            device_id=peer(*peers[n]), device_id_type=MESH)

    def t_copy(n, block):
        piece = right.at[block]
        return pltpu.make_async_remote_copy(
            src_ref=piece, dst_ref=piece, send_sem=t_s.at[n], recv_sem=t_r.at[n],
            device_id=sibling, device_id_type=MESH)

    def square(half, slot):
        left = gath[slot, 0:TOK] if half == 0 else gath2[slot]
        ids = gath[slot, TOK:TOK + TAG].astype(F32)[0:1]
        block = jnp.concatenate([right[slot, 0], right[slot, 1]], axis=1)
        masked = [left * jnp.where(ids == F32(s), F32(1), F32(0)).astype(BF16) for s in range(SEQ_DEV)]
        product = jnp.dot(jnp.concatenate(masked, axis=0), block, preferred_element_type=F32)
        total = None
        for s in range(SEQ_DEV):
            one = product[s * TOK:(s + 1) * TOK]
            total = one * one if total is None else total + one * one
        osum[half, 0] += total[:, :TOK]
        osum[half, 1] += total[:, TOK:]

    def squares(half, r):
        for slot in ring_ga.slots(r):
            square(half, slot)

    def send_partial(half):
        accs[half] = jnp.dot(a_out[...], b_out[half].reshape(HALF, TOK), preferred_element_type=F32)
        psends[half] = accs[half, TOK:].astype(BF16)
        h_copy(1 + half).start()

    def turned(half):
        h_copy(1 + half).wait_recv()
        return (accs[half, :TOK] + precvs[half].astype(F32)).T.astype(BF16)

    for m in range(LAG_B + 9):
        if m <= 8:
            ring_in.step(m)
            ring_a.step(m)
        if m >= LAG_B:
            ring_b.step(m - LAG_B)
        if m == 0:
            y_copy(0).start()
            y_copy(1).start()
        if m == 6:
            y_copy(0).wait_recv()
            k_copy(0, row0).start()
        if m == 7:
            y_copy(1).wait_recv()
            k_copy(1, row0).start()
        if m == 8:
            loads[3].wait()
            k_copy(1, other0).wait_recv()
            send_partial(0)
            loads[2].wait()
            k_copy(0, other0).wait_recv()
            acc[...] = jnp.dot(a_in[...], b_in[...].reshape(HALF, COLS), preferred_element_type=F32)
            psend[...] = acc[TOK:].astype(BF16)
            h_copy(0).start()
        if m == 10:
            gath[z, 0:TOK] = turned(0)
            ring_ga.round(0)
            h_copy(0).wait_recv()
            rotated = (acc[:TOK] + precv[...].astype(F32)).astype(BF16)
            rots[0] = rotated[:, :TOK]
            rots[1] = rotated[:, TOK:]
            for q in range(2):
                p_copy(q).start()
        if m == 11:
            ring_ga.round(1)
            for j in range(2):
                p_arrive(j)
            for n in range(len(peers)):
                q_copy(n, zc).start()
            t_copy(7, zc).start()
        if m == 12:
            ring_ga.round(2)
    send_partial(1)

    for n, (dx, dy) in enumerate(peers):
        block = collected(dx, dy, core)
        q_copy(n, block).wait_recv()
        t_copy(n, block).start()
    ring_ga.round(3)
    for n, (dx, dy) in enumerate(peers):
        t_copy(n, collected(dx, dy, 1 - core)).wait_recv()
    t_copy(7, collected(0, 0, 1 - core)).wait_recv()
    squares(0, 0)
    squares(0, 1)
    gath2[z] = turned(1)
    ring_gb.round(0)
    ring_ga.round(4)
    squares(0, 2)
    squares(0, 3)
    ring_gb.round(1)
    squares(0, 4)
    o_copy(0).start()
    squares(1, 0)
    squares(1, 1)
    for r in range(2, 5):
        ring_gb.round(r)
        squares(1, r)
    o_copy(1).start()

    for ring in (ring_in, ring_a, ring_b, ring_ga, ring_gb):
        ring.finish()
    for i in range(2):
        y_copy(i).wait_send()
        k_copy(i, row0).wait_send()
        p_copy(i).wait_send()
    for i in range(3):
        h_copy(i).wait_send()
    for n, (dx, dy) in enumerate(peers):
        q_copy(n, zc).wait_send()
        t_copy(n, collected(dx, dy, core)).wait_send()
    t_copy(7, zc).wait_send()

    for half in range(2):
        o_copy(half).wait_recv()
        out[half * TOK:(half + 1) * TOK] = (osum[half, h] + orecv[half]) * F32(1.0 / (SEQ_DEV * NZ * NH))
    for half in range(2):
        o_copy(half).wait_send()


def on_device(acts, grads, basis_in, basis_out, seq_ids):
    dma = pltpu.SemaphoreType.DMA
    ring, half, skip = dma((2, 2, 8)), dma((2, 1, 8)), dma((2, 4, 2))
    return pl.pallas_call(
        kernel,
        out_shape=jax.ShapeDtypeStruct((COLS, TOK), F32),
        in_specs=[pl.BlockSpec(memory_space=pl.ANY)] * 4 + [pl.BlockSpec(memory_space=pltpu.VMEM)],
        out_specs=pl.BlockSpec(memory_space=pltpu.VMEM),
        scratch_shapes=[
            pltpu.VMEM((NH * TOK, HALF), BF16),
            pltpu.VMEM((NH * TOK, HALF), BF16),
            pltpu.VMEM((NZ, ROWS, COLS), BF16),
            pltpu.VMEM((2, NZ, ROWS, TOK), BF16),
            pltpu.VMEM((ROWS, COLS), F32),
            pltpu.VMEM((ROWS, COLS), F32),
            pltpu.VMEM((NH * TOK, COLS), F32),
            pltpu.VMEM((2, NH * TOK, TOK), F32),
            pltpu.VMEM((TOK, COLS), BF16),
            pltpu.VMEM((TOK, COLS), BF16),
            pltpu.VMEM((2, TOK, TOK), BF16),
            pltpu.VMEM((2, TOK, TOK), BF16),
            pltpu.VMEM((2, TOK, TOK), BF16),
            pltpu.VMEM((NZ, TOK + TAG, TOK), BF16),
            pltpu.VMEM((NZ, TOK, TOK), BF16),
            pltpu.VMEM((NZ, NH, TOK, TOK), BF16),
            pltpu.VMEM((2, NH, TOK, TOK), F32),
            pltpu.VMEM((2, TOK, TOK), F32),
            dma((4,)),
            ring, ring, half, half, half, half, skip, skip, skip, skip,
            dma((2,)), dma((2,)), dma((2,)), dma((2,)), dma((3,)), dma((3,)),
            dma((2,)), dma((2,)), dma((7,)), dma((7,)), dma((8,)), dma((8,)), dma((2,)), dma((2,)),
        ],
        compiler_params=pltpu.CompilerParams(
            collective_id=0, has_side_effects=True, vmem_limit_bytes=62 * 1024 * 1024),
        cost_estimate=pl.CostEstimate(flops=3_300_000_000, bytes_accessed=8_000_000, transcendentals=0),
    )(acts, grads, basis_in, basis_out, seq_ids.reshape(1, TOK))


def solution(mesh):
    return jax.shard_map(
        on_device,
        mesh=mesh,
        in_specs=(
            P("dp", None),
            P("dp", None),
            P("dp", ("blk", "pair")),
            P("dp", ("blk", "pair")),
            P("dp"),
        ),
        out_specs=P(("blk", "pair"), "dp"),
        check_vma=False,
    )
```

```python
import jax
import jax.numpy as jnp
from jax import lax
from jax.experimental import pallas as pl
from jax.experimental.pallas import tpu as pltpu
from jax.sharding import PartitionSpec as P

SEQ_DEV = 4
TOK = 128
NZ = 16
NH = 2
COLS = 256
ROWS = 256
HALF = NZ * ROWS
LAG_B = 4
TAG = 16
MESH = pl.DeviceIdType.MESH
F32 = jnp.float32
BF16 = jnp.bfloat16


class Ring:
    def __init__(self, piece, hops, send, recv, h, z):
        self.piece, self.hops, self.send, self.recv, self.h, self.z = piece, hops, send, recv, h, z

    def slot(self, way, t):
        return lax.rem(self.z + (NZ - t if way == 0 else t), NZ)

    def copy(self, way, part, t, origin):
        piece = self.piece(part, origin)
        return pltpu.make_async_remote_copy(
            src_ref=piece, dst_ref=piece,
            send_sem=self.send.at[way, part, t], recv_sem=self.recv.at[way, part, t],
            device_id={"dp": self.h * NZ + self.slot(1 - way, 1)}, device_id_type=MESH)

    def step(self, s):
        for part in range(len(self.hops)):
            for way in range(2):
                hops = self.hops[part][way]
                if 1 <= s <= hops:
                    self.copy(way, part, s - 1, self.slot(way, s)).wait_recv()
                if s < hops:
                    self.copy(way, part, s, self.slot(way, s)).start()

    def finish(self):
        for part in range(len(self.hops)):
            for way in range(2):
                for t in range(self.hops[part][way]):
                    self.copy(way, part, t, self.slot(way, t)).wait_send()


class Skip:
    def __init__(self, piece, hops, send, recv, h, z):
        self.piece, self.hops, self.send, self.recv, self.h, self.z = piece, hops, send, recv, h, z

    def slot(self, way, t):
        return lax.rem(self.z + (NZ - t if way == 0 else t), NZ)

    def copy(self, way, r, far, origin):
        piece = self.piece(origin)
        return pltpu.make_async_remote_copy(
            src_ref=piece, dst_ref=piece,
            send_sem=self.send.at[way, r, far], recv_sem=self.recv.at[way, r, far],
            device_id={"dp": self.h * NZ + self.slot(1 - way, 1 + far)}, device_id_type=MESH)

    def round(self, r):
        for way in range(2):
            if r >= 1 and 2 * r <= self.hops[way]:
                self.copy(way, r - 1, 1, self.slot(way, 2 * r)).wait_recv()
            if r < 4:
                for far in (1, 0):
                    if 2 * r + 1 + far <= self.hops[way]:
                        self.copy(way, r, far, self.slot(way, 2 * r)).start()
        if r >= 1:
            for way in range(2):
                self.copy(way, r - 1, 0, self.slot(way, 2 * r - 1)).wait_recv()

    def slots(self, r):
        if r == 0:
            return [self.z]
        near = [self.slot(0, 2 * r - 1), self.slot(1, 2 * r - 1), self.slot(0, 2 * r)]
        return near if r == 4 else near + [self.slot(1, 2 * r)]

    def finish(self):
        for way in range(2):
            for r in range(4):
                for far in range(2):
                    if 2 * r + 1 + far <= self.hops[way]:
                        self.copy(way, r, far, self.slot(way, 2 * r)).wait_send()


def kernel(acts, grads, basis_in, basis_out, seq, out,
           a_in, a_out, b_in, b_out, f_in, f_out, acc, accs, psend, precv, psends, precvs, rots, gath, gath2, right,
           osum, orecv,
           load, in_s, in_r, out_s, out_r, out2_s, out2_r, g_s, g_r, g2_s, g2_r,
           y_s, y_r, x_s, x_r, k_s, k_r, h_s, h_r, p_s, p_r, q_s, q_r, t_s, t_r, o_s, o_r):
    blk, pair, dp = lax.axis_index("blk"), lax.axis_index("pair"), lax.axis_index("dp")
    x, core = blk // 2, lax.rem(blk, 2)
    h, z = dp // NZ, lax.rem(dp, NZ)
    c = blk * 2 + pair
    zc = lax.rem(lax.rem(c, 8) + 7, 8) * 2 + c // 8
    cz = lax.rem(z // 2 + 1, 8) + 8 * lax.rem(z, 2)
    row0 = pl.multiple_of(core * 64, 64)
    other0 = pl.multiple_of((1 - core) * 64, 64)

    across = {"pair": 1 - pair, "dp": (1 - h) * NZ + z}
    twin = {"dp": (1 - h) * NZ + z}
    sibling = {"blk": x * 2 + 1 - core}
    peers = [(dx, dy) for dx in range(4) for dy in range(2) if (dx, dy) != (0, 0)]

    def peer(dx, dy):
        return {"blk": lax.rem(x + dx, 4) * 2 + core, "pair": lax.rem(pair + dy, 2)}

    def collected(dx, dy, k):
        of = (lax.rem(x - dx + 4, 4) * 2 + k) * 2 + lax.rem(pair + dy, 2)
        return lax.rem(lax.rem(of, 8) + 7, 8) * 2 + of // 8

    mine = pl.ds(pl.multiple_of(h * HALF, HALF), HALF)
    theirs = pl.ds(pl.multiple_of((1 - h) * HALF, HALF), HALF)
    loads = [
        pltpu.make_async_copy(basis_in, f_in, load.at[0]),
        pltpu.make_async_copy(basis_out, f_out, load.at[1]),
        pltpu.make_async_copy(acts.at[:, mine], a_in.at[pl.ds(0, TOK)], load.at[2]),
        pltpu.make_async_copy(grads.at[:, mine], a_out.at[pl.ds(0, TOK)], load.at[3]),
    ]
    for one in loads:
        one.start()

    barrier = pltpu.get_barrier_semaphore()
    greet = [
        {"dp": h * NZ + lax.rem(z + 1, NZ)},
        {"dp": h * NZ + lax.rem(z + NZ - 1, NZ)},
        {"dp": h * NZ + lax.rem(z + 2, NZ)},
        {"dp": h * NZ + lax.rem(z + NZ - 2, NZ)},
        across, twin, sibling,
        {"blk": (z // 2) // 2, "pair": lax.rem(z // 2, 2), "dp": h * NZ + zc},
        {"blk": (z // 2) // 2 + 4, "pair": lax.rem(z // 2, 2), "dp": h * NZ + zc},
    ] + [peer(dx, dy) for dx, dy in peers]
    for device in greet:
        pl.semaphore_signal(barrier, inc=1, device_id=device, device_id_type=MESH)

    loads[0].wait()
    b_in[z] = f_in[...].astype(BF16)
    loads[1].wait()
    b_out[0, z] = f_out[:, :TOK].astype(BF16)
    b_out[1, z] = f_out[:, TOK:].astype(BF16)
    tags = jnp.bitwise_and(seq[...], SEQ_DEV - 1).astype(F32)
    gath[z, TOK:TOK + TAG] = jnp.broadcast_to(tags, (TAG, TOK)).astype(BF16)
    osum[...] = jnp.zeros_like(osum)

    pl.semaphore_wait(barrier, len(greet))

    part_rows = ROWS // 2
    ring_in = Ring(lambda part, slot: b_in.at[slot, pl.ds(part * part_rows, part_rows)],
                   ((8, 7), (7, 8)), in_s, in_r, h, z)
    ring_a = Ring(lambda part, slot: b_out.at[0, slot], ((8, 7),), out_s, out_r, h, z)
    ring_b = Ring(lambda part, slot: b_out.at[1, slot], ((7, 8),), out2_s, out2_r, h, z)
    ring_ga = Skip(lambda slot: gath.at[slot], (8, 7), g_s, g_r, h, z)
    ring_gb = Skip(lambda slot: gath2.at[slot], (7, 8), g2_s, g2_r, h, z)

    def yrow(dx):
        return pl.multiple_of(core * 64 + lax.rem(x - dx + 4, 4) * 16, 16)

    def x_copy(i, dx, first):
        piece = (a_in, a_out)[i].at[pl.ds(TOK + first, 16)]
        return pltpu.make_async_remote_copy(
            src_ref=piece, dst_ref=piece, send_sem=x_s.at[i, dx - 1], recv_sem=x_r.at[i, dx - 1],
            device_id=peer(dx, 0), device_id_type=MESH)

    def y_copy(i):
        source, held = ((acts, a_in), (grads, a_out))[i]
        return pltpu.make_async_remote_copy(
            src_ref=source.at[pl.ds(yrow(0), 16), theirs], dst_ref=held.at[pl.ds(TOK + yrow(0), 16)],
            send_sem=y_s.at[i], recv_sem=y_r.at[i], device_id=across, device_id_type=MESH)

    def k_copy(i, first):
        piece = (a_in, a_out)[i].at[pl.ds(TOK + first, 64)]
        return pltpu.make_async_remote_copy(
            src_ref=piece, dst_ref=piece, send_sem=k_s.at[i], recv_sem=k_r.at[i],
            device_id=sibling, device_id_type=MESH)

    def h_copy(i):
        source, target = (psend, precv) if i == 0 else (psends.at[i - 1], precvs.at[i - 1])
        return pltpu.make_async_remote_copy(
            src_ref=source, dst_ref=target, send_sem=h_s.at[i], recv_sem=h_r.at[i],
            device_id=twin, device_id_type=MESH)

    def o_copy(half):
        return pltpu.make_async_remote_copy(
            src_ref=osum.at[half, 1 - h], dst_ref=orecv.at[half], send_sem=o_s.at[half], recv_sem=o_r.at[half],
            device_id=twin, device_id_type=MESH)

    def p_copy(q):
        return pltpu.make_async_remote_copy(
            src_ref=rots.at[q], dst_ref=right.at[z, c // 8], send_sem=p_s.at[q], recv_sem=p_r.at[c // 8],
            device_id={"blk": cz // 2, "pair": lax.rem(cz, 2), "dp": h * NZ + 2 * lax.rem(c, 8) + q},
            device_id_type=MESH)

    def p_arrive(j):
        piece = right.at[zc, j]
        pltpu.make_async_remote_copy(
            src_ref=piece, dst_ref=piece, send_sem=p_s.at[0], recv_sem=p_r.at[j],
            device_id=twin, device_id_type=MESH).wait_recv()

    def q_copy(n, block):
        piece = right.at[block]
        return pltpu.make_async_remote_copy(
            src_ref=piece, dst_ref=piece, send_sem=q_s.at[n], recv_sem=q_r.at[n],
            device_id=peer(*peers[n]), device_id_type=MESH)

    def t_copy(n, block):
        piece = right.at[block]
        return pltpu.make_async_remote_copy(
            src_ref=piece, dst_ref=piece, send_sem=t_s.at[n], recv_sem=t_r.at[n],
            device_id=sibling, device_id_type=MESH)

    def square(half, slot):
        left = gath[slot, 0:TOK] if half == 0 else gath2[slot]
        ids = gath[slot, TOK:TOK + TAG].astype(F32)[0:1]
        block = jnp.concatenate([right[slot, 0], right[slot, 1]], axis=1)
        masked = [left * jnp.where(ids == F32(s), F32(1), F32(0)).astype(BF16) for s in range(SEQ_DEV)]
        product = jnp.dot(jnp.concatenate(masked, axis=0), block, preferred_element_type=F32)
        total = None
        for s in range(SEQ_DEV):
            one = product[s * TOK:(s + 1) * TOK]
            total = one * one if total is None else total + one * one
        osum[half, 0] += total[:, :TOK]
        osum[half, 1] += total[:, TOK:]

    def squares(half, r):
        for slot in ring_ga.slots(r):
            square(half, slot)

    def send_partial(half):
        accs[half] = jnp.dot(a_out[...], b_out[half].reshape(HALF, TOK), preferred_element_type=F32)
        psends[half] = accs[half, TOK:].astype(BF16)
        h_copy(1 + half).start()

    def turned(half):
        h_copy(1 + half).wait_recv()
        return (accs[half, :TOK] + precvs[half].astype(F32)).T.astype(BF16)

    for m in range(LAG_B + 9):
        if m <= 8:
            ring_in.step(m)
            ring_a.step(m)
        if m >= LAG_B:
            ring_b.step(m - LAG_B)
        if m == 0:
            y_copy(0).start()
            y_copy(1).start()
        if m == 3:
            for i in range(2):
                y_copy(i).wait_recv()
                for dx in range(1, 4):
                    x_copy(i, dx, yrow(0)).start()
        if m == 6:
            for i in range(2):
                for dx in range(1, 4):
                    x_copy(i, dx, yrow(dx)).wait_recv()
                k_copy(i, row0).start()
        if m == 8:
            loads[3].wait()
            k_copy(1, other0).wait_recv()
            send_partial(0)
            loads[2].wait()
            k_copy(0, other0).wait_recv()
            acc[...] = jnp.dot(a_in[...], b_in[...].reshape(HALF, COLS), preferred_element_type=F32)
            psend[...] = acc[TOK:].astype(BF16)
            h_copy(0).start()
        if m == 10:
            gath[z, 0:TOK] = turned(0)
            ring_ga.round(0)
            h_copy(0).wait_recv()
            rotated = (acc[:TOK] + precv[...].astype(F32)).astype(BF16)
            rots[0] = rotated[:, :TOK]
            rots[1] = rotated[:, TOK:]
            for q in range(2):
                p_copy(q).start()
        if m == 11:
            ring_ga.round(1)
            for j in range(2):
                p_arrive(j)
            for n in range(len(peers)):
                q_copy(n, zc).start()
            t_copy(7, zc).start()
        if m == 12:
            ring_ga.round(2)
    send_partial(1)

    for n, (dx, dy) in enumerate(peers):
        block = collected(dx, dy, core)
        q_copy(n, block).wait_recv()
        t_copy(n, block).start()
    ring_ga.round(3)
    for n, (dx, dy) in enumerate(peers):
        t_copy(n, collected(dx, dy, 1 - core)).wait_recv()
    t_copy(7, collected(0, 0, 1 - core)).wait_recv()
    squares(0, 0)
    squares(0, 1)
    gath2[z] = turned(1)
    ring_gb.round(0)
    ring_ga.round(4)
    squares(0, 2)
    squares(0, 3)
    ring_gb.round(1)
    squares(0, 4)
    o_copy(0).start()
    squares(1, 0)
    squares(1, 1)
    for r in range(2, 5):
        ring_gb.round(r)
        squares(1, r)
    o_copy(1).start()

    for ring in (ring_in, ring_a, ring_b, ring_ga, ring_gb):
        ring.finish()
    for i in range(2):
        y_copy(i).wait_send()
        for dx in range(1, 4):
            x_copy(i, dx, yrow(0)).wait_send()
        k_copy(i, row0).wait_send()
        p_copy(i).wait_send()
    for i in range(3):
        h_copy(i).wait_send()
    for n, (dx, dy) in enumerate(peers):
        q_copy(n, zc).wait_send()
        t_copy(n, collected(dx, dy, core)).wait_send()
    t_copy(7, zc).wait_send()

    for half in range(2):
        o_copy(half).wait_recv()
        out[half * TOK:(half + 1) * TOK] = (osum[half, h] + orecv[half]) * F32(1.0 / (SEQ_DEV * NZ * NH))
    for half in range(2):
        o_copy(half).wait_send()


def on_device(acts, grads, basis_in, basis_out, seq_ids):
    dma = pltpu.SemaphoreType.DMA
    ring, half, skip = dma((2, 2, 8)), dma((2, 1, 8)), dma((2, 4, 2))
    return pl.pallas_call(
        kernel,
        out_shape=jax.ShapeDtypeStruct((COLS, TOK), F32),
        in_specs=[pl.BlockSpec(memory_space=pl.ANY)] * 4 + [pl.BlockSpec(memory_space=pltpu.VMEM)],
        out_specs=pl.BlockSpec(memory_space=pltpu.VMEM),
        scratch_shapes=[
            pltpu.VMEM((NH * TOK, HALF), BF16),
            pltpu.VMEM((NH * TOK, HALF), BF16),
            pltpu.VMEM((NZ, ROWS, COLS), BF16),
            pltpu.VMEM((2, NZ, ROWS, TOK), BF16),
            pltpu.VMEM((ROWS, COLS), F32),
            pltpu.VMEM((ROWS, COLS), F32),
            pltpu.VMEM((NH * TOK, COLS), F32),
            pltpu.VMEM((2, NH * TOK, TOK), F32),
            pltpu.VMEM((TOK, COLS), BF16),
            pltpu.VMEM((TOK, COLS), BF16),
            pltpu.VMEM((2, TOK, TOK), BF16),
            pltpu.VMEM((2, TOK, TOK), BF16),
            pltpu.VMEM((2, TOK, TOK), BF16),
            pltpu.VMEM((NZ, TOK + TAG, TOK), BF16),
            pltpu.VMEM((NZ, TOK, TOK), BF16),
            pltpu.VMEM((NZ, NH, TOK, TOK), BF16),
            pltpu.VMEM((2, NH, TOK, TOK), F32),
            pltpu.VMEM((2, TOK, TOK), F32),
            dma((4,)),
            ring, ring, half, half, half, half, skip, skip, skip, skip,
            dma((2,)), dma((2,)), dma((2, 3)), dma((2, 3)), dma((2,)), dma((2,)), dma((3,)), dma((3,)),
            dma((2,)), dma((2,)), dma((7,)), dma((7,)), dma((8,)), dma((8,)), dma((2,)), dma((2,)),
        ],
        compiler_params=pltpu.CompilerParams(
            collective_id=0, has_side_effects=True, vmem_limit_bytes=62 * 1024 * 1024),
        cost_estimate=pl.CostEstimate(flops=3_300_000_000, bytes_accessed=8_000_000, transcendentals=0),
    )(acts, grads, basis_in, basis_out, seq_ids.reshape(1, TOK))


def solution(mesh):
    return jax.shard_map(
        on_device,
        mesh=mesh,
        in_specs=(
            P("dp", None),
            P("dp", None),
            P("dp", ("blk", "pair")),
            P("dp", ("blk", "pair")),
            P("dp"),
        ),
        out_specs=P(("blk", "pair"), "dp"),
        check_vma=False,
    )
```

```python
import jax
import jax.numpy as jnp
from jax import lax
from jax.experimental import pallas as pl
from jax.experimental.pallas import tpu as pltpu
from jax.sharding import PartitionSpec as P

SEQ_DEV = 4
TOK = 128
NZ = 16
NH = 2
COLS = 256
ROWS = 256
HALF = NZ * ROWS
LAG_B = 4
TAG = 16
MESH = pl.DeviceIdType.MESH
F32 = jnp.float32
BF16 = jnp.bfloat16


class Ring:
    def __init__(self, piece, hops, send, recv, h, z):
        self.piece, self.hops, self.send, self.recv, self.h, self.z = piece, hops, send, recv, h, z

    def slot(self, way, t):
        return lax.rem(self.z + (NZ - t if way == 0 else t), NZ)

    def copy(self, way, part, t, origin):
        piece = self.piece(part, origin)
        return pltpu.make_async_remote_copy(
            src_ref=piece, dst_ref=piece,
            send_sem=self.send.at[way, part, t], recv_sem=self.recv.at[way, part, t],
            device_id={"dp": self.h * NZ + self.slot(1 - way, 1)}, device_id_type=MESH)

    def step(self, s):
        for part in range(len(self.hops)):
            for way in range(2):
                hops = self.hops[part][way]
                if 1 <= s <= hops:
                    self.copy(way, part, s - 1, self.slot(way, s)).wait_recv()
                if s < hops:
                    self.copy(way, part, s, self.slot(way, s)).start()

    def finish(self):
        for part in range(len(self.hops)):
            for way in range(2):
                for t in range(self.hops[part][way]):
                    self.copy(way, part, t, self.slot(way, t)).wait_send()


class Skip:
    def __init__(self, piece, hops, send, recv, h, z):
        self.piece, self.hops, self.send, self.recv, self.h, self.z = piece, hops, send, recv, h, z

    def slot(self, way, t):
        return lax.rem(self.z + (NZ - t if way == 0 else t), NZ)

    def copy(self, way, r, far, origin):
        piece = self.piece(origin)
        return pltpu.make_async_remote_copy(
            src_ref=piece, dst_ref=piece,
            send_sem=self.send.at[way, r, far], recv_sem=self.recv.at[way, r, far],
            device_id={"dp": self.h * NZ + self.slot(1 - way, 1 + far)}, device_id_type=MESH)

    def round(self, r):
        for way in range(2):
            if r >= 1 and 2 * r <= self.hops[way]:
                self.copy(way, r - 1, 1, self.slot(way, 2 * r)).wait_recv()
            if r < 4:
                for far in (1, 0):
                    if 2 * r + 1 + far <= self.hops[way]:
                        self.copy(way, r, far, self.slot(way, 2 * r)).start()
        if r >= 1:
            for way in range(2):
                self.copy(way, r - 1, 0, self.slot(way, 2 * r - 1)).wait_recv()

    def slots(self, r):
        if r == 0:
            return [self.z]
        near = [self.slot(0, 2 * r - 1), self.slot(1, 2 * r - 1), self.slot(0, 2 * r)]
        return near if r == 4 else near + [self.slot(1, 2 * r)]

    def finish(self):
        for way in range(2):
            for r in range(4):
                for far in range(2):
                    if 2 * r + 1 + far <= self.hops[way]:
                        self.copy(way, r, far, self.slot(way, 2 * r)).wait_send()


def kernel(acts, grads, basis_in, basis_out, seq, out,
           a_in, a_out, b_in, b_out, f_in, f_out, acc, accs, psend, precv, psends, precvs, rots, gath, gath2, right,
           osum, orecv,
           load, in_s, in_r, out_s, out_r, out2_s, out2_r, g_s, g_r, g2_s, g2_r,
           y_s, y_r, k_s, k_r, h_s, h_r, p_s, p_r, q_s, q_r, t_s, t_r, o_s, o_r):
    blk, pair, dp = lax.axis_index("blk"), lax.axis_index("pair"), lax.axis_index("dp")
    x, core = blk // 2, lax.rem(blk, 2)
    h, z = dp // NZ, lax.rem(dp, NZ)
    c = blk * 2 + pair
    zc = lax.rem(lax.rem(c, 8) + 7, 8) * 2 + c // 8
    cz = lax.rem(z // 2 + 1, 8) + 8 * lax.rem(z, 2)
    row0 = pl.multiple_of(core * 64, 64)
    other0 = pl.multiple_of((1 - core) * 64, 64)

    across = {"pair": 1 - pair, "dp": (1 - h) * NZ + z}
    twin = {"dp": (1 - h) * NZ + z}
    sibling = {"blk": x * 2 + 1 - core}
    peers = [(dx, dy) for dx in range(4) for dy in range(2) if (dx, dy) != (0, 0)]

    def peer(dx, dy):
        return {"blk": lax.rem(x + dx, 4) * 2 + core, "pair": lax.rem(pair + dy, 2)}

    def collected(dx, dy, k):
        of = (lax.rem(x - dx + 4, 4) * 2 + k) * 2 + lax.rem(pair + dy, 2)
        return lax.rem(lax.rem(of, 8) + 7, 8) * 2 + of // 8

    mine = pl.ds(pl.multiple_of(h * HALF, HALF), HALF)
    theirs = pl.ds(pl.multiple_of((1 - h) * HALF, HALF), HALF)
    loads = [
        pltpu.make_async_copy(basis_in, f_in, load.at[0]),
        pltpu.make_async_copy(basis_out, f_out, load.at[1]),
        pltpu.make_async_copy(acts.at[:, mine], a_in.at[pl.ds(0, TOK)], load.at[2]),
        pltpu.make_async_copy(grads.at[:, mine], a_out.at[pl.ds(0, TOK)], load.at[3]),
    ]
    for one in loads:
        one.start()

    barrier = pltpu.get_barrier_semaphore()
    greet = [
        {"dp": h * NZ + lax.rem(z + 1, NZ)},
        {"dp": h * NZ + lax.rem(z + NZ - 1, NZ)},
        {"dp": h * NZ + lax.rem(z + 2, NZ)},
        {"dp": h * NZ + lax.rem(z + NZ - 2, NZ)},
        across, twin, sibling,
        {"blk": (z // 2) // 2, "pair": lax.rem(z // 2, 2), "dp": h * NZ + zc},
        {"blk": (z // 2) // 2 + 4, "pair": lax.rem(z // 2, 2), "dp": h * NZ + zc},
    ] + [peer(dx, dy) for dx, dy in peers]
    for device in greet:
        pl.semaphore_signal(barrier, inc=1, device_id=device, device_id_type=MESH)

    loads[0].wait()
    b_in[z] = f_in[...].astype(BF16)
    loads[1].wait()
    b_out[0, z] = f_out[:, :TOK].astype(BF16)
    b_out[1, z] = f_out[:, TOK:].astype(BF16)
    tags = jnp.bitwise_and(seq[...], SEQ_DEV - 1).astype(F32)
    gath[z, TOK:TOK + TAG] = jnp.broadcast_to(tags, (TAG, TOK)).astype(BF16)
    osum[...] = jnp.zeros_like(osum)
    acc[...] = jnp.zeros_like(acc)
    accs[...] = jnp.zeros_like(accs)

    pl.semaphore_wait(barrier, len(greet))

    ring_in = Ring(lambda part, slot: b_in.at[slot], ((8, 7),), in_s, in_r, h, z)
    ring_a = Ring(lambda part, slot: b_out.at[0, slot], ((7, 8),), out_s, out_r, h, z)
    ring_b = Ring(lambda part, slot: b_out.at[1, slot], ((7, 8),), out2_s, out2_r, h, z)
    ring_ga = Skip(lambda slot: gath.at[slot], (8, 7), g_s, g_r, h, z)
    ring_gb = Skip(lambda slot: gath2.at[slot], (7, 8), g2_s, g2_r, h, z)

    def y_copy(i):
        source, held = ((acts, a_in), (grads, a_out))[i]
        return pltpu.make_async_remote_copy(
            src_ref=source.at[pl.ds(row0, 64), theirs], dst_ref=held.at[pl.ds(TOK + row0, 64)],
            send_sem=y_s.at[i], recv_sem=y_r.at[i], device_id=across, device_id_type=MESH)

    def k_copy(i, first):
        piece = (a_in, a_out)[i].at[pl.ds(TOK + first, 64)]
        return pltpu.make_async_remote_copy(
            src_ref=piece, dst_ref=piece, send_sem=k_s.at[i], recv_sem=k_r.at[i],
            device_id=sibling, device_id_type=MESH)

    def h_copy(i):
        source, target = (psend, precv) if i == 0 else (psends.at[i - 1], precvs.at[i - 1])
        return pltpu.make_async_remote_copy(
            src_ref=source, dst_ref=target, send_sem=h_s.at[i], recv_sem=h_r.at[i],
            device_id=twin, device_id_type=MESH)

    def o_copy(half):
        return pltpu.make_async_remote_copy(
            src_ref=osum.at[half, 1 - h], dst_ref=orecv.at[half], send_sem=o_s.at[half], recv_sem=o_r.at[half],
            device_id=twin, device_id_type=MESH)

    def p_copy(q):
        return pltpu.make_async_remote_copy(
            src_ref=rots.at[q], dst_ref=right.at[z, c // 8], send_sem=p_s.at[q], recv_sem=p_r.at[c // 8],
            device_id={"blk": cz // 2, "pair": lax.rem(cz, 2), "dp": h * NZ + 2 * lax.rem(c, 8) + q},
            device_id_type=MESH)

    def p_arrive(j):
        piece = right.at[zc, j]
        pltpu.make_async_remote_copy(
            src_ref=piece, dst_ref=piece, send_sem=p_s.at[0], recv_sem=p_r.at[j],
            device_id=twin, device_id_type=MESH).wait_recv()

    def q_copy(n, block):
        piece = right.at[block]
        return pltpu.make_async_remote_copy(
            src_ref=piece, dst_ref=piece, send_sem=q_s.at[n], recv_sem=q_r.at[n],
            device_id=peer(*peers[n]), device_id_type=MESH)

    def t_copy(n, block):
        piece = right.at[block]
        return pltpu.make_async_remote_copy(
            src_ref=piece, dst_ref=piece, send_sem=t_s.at[n], recv_sem=t_r.at[n],
            device_id=sibling, device_id_type=MESH)

    def add_in(slot):
        columns = pl.ds(pl.multiple_of(slot * ROWS, ROWS), ROWS)
        acc[...] += jnp.dot(a_in[:, columns], b_in[slot], preferred_element_type=F32)

    def add_out(half, slot):
        columns = pl.ds(pl.multiple_of(slot * ROWS, ROWS), ROWS)
        accs[half] += jnp.dot(a_out[:, columns], b_out[half, slot], preferred_element_type=F32)

    def around(near, far, add):
        @pl.loop(2 * near, 2 * far + 2)
        def _(n):
            add(lax.rem(z + NZ + (2 * lax.rem(n, 2) - 1) * (n // 2), NZ))

    def add_a(slot):
        add_out(0, slot)

    def add_b(slot):
        add_out(1, slot)

    opposite = lax.rem(z + NZ // 2, NZ)

    def square(half, slot):
        left = gath[slot, 0:TOK] if half == 0 else gath2[slot]
        ids = gath[slot, TOK:TOK + TAG].astype(F32)[0:1]
        block = jnp.concatenate([right[slot, 0], right[slot, 1]], axis=1)
        masked = [left * jnp.where(ids == F32(s), F32(1), F32(0)).astype(BF16) for s in range(SEQ_DEV)]
        product = jnp.dot(jnp.concatenate(masked, axis=0), block, preferred_element_type=F32)
        total = None
        for s in range(SEQ_DEV):
            one = product[s * TOK:(s + 1) * TOK]
            total = one * one if total is None else total + one * one
        osum[half, 0] += total[:, :TOK]
        osum[half, 1] += total[:, TOK:]

    def squares(half, r):
        for slot in ring_ga.slots(r):
            square(half, slot)

    def send_partial(half):
        psends[half] = accs[half, TOK:].astype(BF16)
        h_copy(1 + half).start()

    def turned(half):
        h_copy(1 + half).wait_recv()
        return (accs[half, :TOK] + precvs[half].astype(F32)).T.astype(BF16)

    for m in range(LAG_B + 9):
        if m <= 8:
            ring_in.step(m)
            ring_a.step(m)
        if m >= LAG_B:
            ring_b.step(m - LAG_B)
        if m == 0:
            y_copy(0).start()
            y_copy(1).start()
        if m == 6:
            for i in (1, 0):
                y_copy(i).wait_recv()
                k_copy(i, row0).start()
        if m == 7:
            loads[3].wait()
            k_copy(1, other0).wait_recv()
            add_a(z)
            around(1, 4, add_a)
            loads[2].wait()
            k_copy(0, other0).wait_recv()
            add_in(z)
            around(1, 4, add_in)
        if m == 8:
            around(5, 7, add_a)
            add_a(opposite)
            send_partial(0)
            around(5, 7, add_in)
            add_in(opposite)
            psend[...] = acc[TOK:].astype(BF16)
            h_copy(0).start()
        if m == 9:
            add_b(z)
            around(1, 4, add_b)
            ring_in.finish()
        if m == 10:
            gath[z, 0:TOK] = turned(0)
            ring_ga.round(0)
            h_copy(0).wait_recv()
            rotated = (acc[:TOK] + precv[...].astype(F32)).astype(BF16)
            rots[0] = rotated[:, :TOK]
            rots[1] = rotated[:, TOK:]
            for q in range(2):
                p_copy(q).start()
        if m == 11:
            ring_ga.round(1)
            for j in range(2):
                p_arrive(j)
            for n in range(len(peers)):
                q_copy(n, zc).start()
            t_copy(7, zc).start()
            around(5, 6, add_b)
        if m == 12:
            around(7, 7, add_b)
            add_b(opposite)
            send_partial(1)
            ring_ga.round(2)

    for n, (dx, dy) in enumerate(peers):
        block = collected(dx, dy, core)
        q_copy(n, block).wait_recv()
        t_copy(n, block).start()
    ring_ga.round(3)
    gath2[z] = turned(1)
    ring_gb.round(0)
    for n, (dx, dy) in enumerate(peers):
        t_copy(n, collected(dx, dy, 1 - core)).wait_recv()
    t_copy(7, collected(0, 0, 1 - core)).wait_recv()
    squares(0, 0)
    squares(0, 1)
    ring_ga.round(4)
    squares(0, 2)
    ring_gb.round(1)
    squares(0, 3)
    squares(0, 4)
    o_copy(0).start()
    squares(1, 0)
    ring_gb.round(2)
    squares(1, 1)
    ring_a.finish()
    ring_gb.round(3)
    squares(1, 2)
    for i in range(2):
        y_copy(i).wait_send()
        k_copy(i, row0).wait_send()
        p_copy(i).wait_send()
    for i in range(3):
        h_copy(i).wait_send()
    ring_gb.round(4)
    squares(1, 3)
    squares(1, 4)
    o_copy(1).start()

    ring_b.finish()
    ring_ga.finish()
    ring_gb.finish()
    for n, (dx, dy) in enumerate(peers):
        q_copy(n, zc).wait_send()
        t_copy(n, collected(dx, dy, core)).wait_send()
    t_copy(7, zc).wait_send()

    for half in range(2):
        o_copy(half).wait_recv()
        out[half * TOK:(half + 1) * TOK] = (osum[half, h] + orecv[half]) * F32(1.0 / (SEQ_DEV * NZ * NH))
    for half in range(2):
        o_copy(half).wait_send()


def on_device(acts, grads, basis_in, basis_out, seq_ids):
    dma = pltpu.SemaphoreType.DMA
    half, skip = dma((2, 1, 8)), dma((2, 4, 2))
    return pl.pallas_call(
        kernel,
        out_shape=jax.ShapeDtypeStruct((COLS, TOK), F32),
        in_specs=[pl.BlockSpec(memory_space=pl.ANY)] * 4 + [pl.BlockSpec(memory_space=pltpu.VMEM)],
        out_specs=pl.BlockSpec(memory_space=pltpu.VMEM),
        scratch_shapes=[
            pltpu.VMEM((NH * TOK, HALF), BF16),
            pltpu.VMEM((NH * TOK, HALF), BF16),
            pltpu.VMEM((NZ, ROWS, COLS), BF16),
            pltpu.VMEM((2, NZ, ROWS, TOK), BF16),
            pltpu.VMEM((ROWS, COLS), F32),
            pltpu.VMEM((ROWS, COLS), F32),
            pltpu.VMEM((NH * TOK, COLS), F32),
            pltpu.VMEM((2, NH * TOK, TOK), F32),
            pltpu.VMEM((TOK, COLS), BF16),
            pltpu.VMEM((TOK, COLS), BF16),
            pltpu.VMEM((2, TOK, TOK), BF16),
            pltpu.VMEM((2, TOK, TOK), BF16),
            pltpu.VMEM((2, TOK, TOK), BF16),
            pltpu.VMEM((NZ, TOK + TAG, TOK), BF16),
            pltpu.VMEM((NZ, TOK, TOK), BF16),
            pltpu.VMEM((NZ, NH, TOK, TOK), BF16),
            pltpu.VMEM((2, NH, TOK, TOK), F32),
            pltpu.VMEM((2, TOK, TOK), F32),
            dma((4,)),
            half, half, half, half, half, half, skip, skip, skip, skip,
            dma((2,)), dma((2,)), dma((2,)), dma((2,)), dma((3,)), dma((3,)),
            dma((2,)), dma((2,)), dma((7,)), dma((7,)), dma((8,)), dma((8,)), dma((2,)), dma((2,)),
        ],
        compiler_params=pltpu.CompilerParams(
            collective_id=0, has_side_effects=True, vmem_limit_bytes=62 * 1024 * 1024),
        cost_estimate=pl.CostEstimate(flops=3_300_000_000, bytes_accessed=8_000_000, transcendentals=0),
    )(acts, grads, basis_in, basis_out, seq_ids.reshape(1, TOK))


def solution(mesh):
    return jax.shard_map(
        on_device,
        mesh=mesh,
        in_specs=(
            P("dp", None),
            P("dp", None),
            P("dp", ("blk", "pair")),
            P("dp", ("blk", "pair")),
            P("dp"),
        ),
        out_specs=P(("blk", "pair"), "dp"),
        check_vma=False,
    )
```

```python
import jax
import jax.numpy as jnp
from jax import lax
from jax.experimental import pallas as pl
from jax.experimental.pallas import tpu as pltpu
from jax.sharding import PartitionSpec as P

SEQ_DEV = 4
TOK = 128
NZ = 16
NH = 2
COLS = 256
ROWS = 256
HALF = NZ * ROWS
LAG_A = 2
LAG_B = 5
TAG = 16
MESH = pl.DeviceIdType.MESH
F32 = jnp.float32
BF16 = jnp.bfloat16


class Ring:
    def __init__(self, piece, hops, send, recv, h, z):
        self.piece, self.hops, self.send, self.recv, self.h, self.z = piece, hops, send, recv, h, z

    def slot(self, way, t):
        return lax.rem(self.z + (NZ - t if way == 0 else t), NZ)

    def copy(self, way, part, t, origin):
        piece = self.piece(part, origin)
        return pltpu.make_async_remote_copy(
            src_ref=piece, dst_ref=piece,
            send_sem=self.send.at[way, part, t], recv_sem=self.recv.at[way, part, t],
            device_id={"dp": self.h * NZ + self.slot(1 - way, 1)}, device_id_type=MESH)

    def step(self, s):
        for part in range(len(self.hops)):
            for way in range(2):
                hops = self.hops[part][way]
                if 1 <= s <= hops:
                    self.copy(way, part, s - 1, self.slot(way, s)).wait_recv()
                if s < hops:
                    self.copy(way, part, s, self.slot(way, s)).start()

    def finish(self):
        for part in range(len(self.hops)):
            for way in range(2):
                for t in range(self.hops[part][way]):
                    self.copy(way, part, t, self.slot(way, t)).wait_send()


class Skip:
    def __init__(self, piece, hops, send, recv, h, z):
        self.piece, self.hops, self.send, self.recv, self.h, self.z = piece, hops, send, recv, h, z

    def slot(self, way, t):
        return lax.rem(self.z + (NZ - t if way == 0 else t), NZ)

    def copy(self, way, r, far, origin):
        piece = self.piece(origin)
        return pltpu.make_async_remote_copy(
            src_ref=piece, dst_ref=piece,
            send_sem=self.send.at[way, r, far], recv_sem=self.recv.at[way, r, far],
            device_id={"dp": self.h * NZ + self.slot(1 - way, 1 + far)}, device_id_type=MESH)

    def round(self, r):
        for way in range(2):
            if r >= 1 and 2 * r <= self.hops[way]:
                self.copy(way, r - 1, 1, self.slot(way, 2 * r)).wait_recv()
            if r < 4:
                for far in (1, 0):
                    if 2 * r + 1 + far <= self.hops[way]:
                        self.copy(way, r, far, self.slot(way, 2 * r)).start()
        if r >= 1:
            for way in range(2):
                self.copy(way, r - 1, 0, self.slot(way, 2 * r - 1)).wait_recv()

    def slots(self, r):
        if r == 0:
            return [self.z]
        near = [self.slot(0, 2 * r - 1), self.slot(1, 2 * r - 1), self.slot(0, 2 * r)]
        return near if r == 4 else near + [self.slot(1, 2 * r)]

    def finish(self):
        for way in range(2):
            for r in range(4):
                for far in range(2):
                    if 2 * r + 1 + far <= self.hops[way]:
                        self.copy(way, r, far, self.slot(way, 2 * r)).wait_send()


def kernel(acts, grads, basis_in, basis_out, seq, out,
           a_in, a_out, b_in, b_out, f_in, f_out, acc, accs, psend, precv, psends, precvs, rots, gath, gath2, right,
           osum, orecv,
           load, in_s, in_r, out_s, out_r, out2_s, out2_r, g_s, g_r, g2_s, g2_r,
           y_s, y_r, k_s, k_r, h_s, h_r, p_s, p_r, q_s, q_r, t_s, t_r, o_s, o_r):
    blk, pair, dp = lax.axis_index("blk"), lax.axis_index("pair"), lax.axis_index("dp")
    x, core = blk // 2, lax.rem(blk, 2)
    h, z = dp // NZ, lax.rem(dp, NZ)
    c = blk * 2 + pair
    zc = lax.rem(c + z // 2 + NZ - 2, NZ)
    cz = lax.rem(z - lax.rem(c, 8) + 2 + NZ, NZ)
    row0 = pl.multiple_of(core * 64, 64)
    other0 = pl.multiple_of((1 - core) * 64, 64)

    across = {"pair": 1 - pair, "dp": (1 - h) * NZ + z}
    twin = {"dp": (1 - h) * NZ + z}
    sibling = {"blk": x * 2 + 1 - core}
    peers = [(dx, dy) for dx in range(4) for dy in range(2) if (dx, dy) != (0, 0)]

    def peer(dx, dy):
        return {"blk": lax.rem(x + dx, 4) * 2 + core, "pair": lax.rem(pair + dy, 2)}

    def collected(dx, dy, k):
        of = (lax.rem(x - dx + 4, 4) * 2 + k) * 2 + lax.rem(pair + dy, 2)
        return lax.rem(of + z // 2 + NZ - 2, NZ)

    mine = pl.ds(pl.multiple_of(h * HALF, HALF), HALF)
    theirs = pl.ds(pl.multiple_of((1 - h) * HALF, HALF), HALF)
    loads = [
        pltpu.make_async_copy(basis_in, f_in, load.at[0]),
        pltpu.make_async_copy(basis_out, f_out, load.at[1]),
        pltpu.make_async_copy(acts.at[:, mine], a_in.at[pl.ds(0, TOK)], load.at[2]),
        pltpu.make_async_copy(grads.at[:, mine], a_out.at[pl.ds(0, TOK)], load.at[3]),
    ]
    for one in loads:
        one.start()

    barrier = pltpu.get_barrier_semaphore()
    greet = [
        {"dp": h * NZ + lax.rem(z + 1, NZ)},
        {"dp": h * NZ + lax.rem(z + NZ - 1, NZ)},
        {"dp": h * NZ + lax.rem(z + 2, NZ)},
        {"dp": h * NZ + lax.rem(z + NZ - 2, NZ)},
        across, twin, sibling,
        {"blk": (z // 2) // 2, "pair": lax.rem(z // 2, 2), "dp": h * NZ + zc},
        {"blk": (z // 2) // 2 + 4, "pair": lax.rem(z // 2, 2), "dp": h * NZ + zc},
    ] + [peer(dx, dy) for dx, dy in peers]
    for device in greet:
        pl.semaphore_signal(barrier, inc=1, device_id=device, device_id_type=MESH)

    loads[0].wait()
    b_in[z] = f_in[...].astype(BF16)
    loads[1].wait()
    b_out[0, z] = f_out[:, :TOK].astype(BF16)
    b_out[1, z] = f_out[:, TOK:].astype(BF16)
    tags = jnp.bitwise_and(seq[...], SEQ_DEV - 1).astype(F32)
    gath[z, TOK:TOK + TAG] = jnp.broadcast_to(tags, (TAG, TOK)).astype(BF16)
    osum[...] = jnp.zeros_like(osum)
    acc[...] = jnp.zeros_like(acc)
    accs[...] = jnp.zeros_like(accs)

    pl.semaphore_wait(barrier, len(greet))

    part_rows = ROWS // 2
    ring_in = Ring(lambda part, slot: b_in.at[slot, pl.ds(part * part_rows, part_rows)],
                   ((8, 7), (7, 8)), in_s, in_r, h, z)
    ring_a = Ring(lambda part, slot: b_out.at[0, slot], ((8, 7),), out_s, out_r, h, z)
    ring_b = Ring(lambda part, slot: b_out.at[1, slot], ((7, 8),), out2_s, out2_r, h, z)
    ring_ga = Skip(lambda slot: gath.at[slot], (8, 7), g_s, g_r, h, z)
    ring_gb = Skip(lambda slot: gath2.at[slot], (7, 8), g2_s, g2_r, h, z)

    def y_copy(i):
        source, held = ((acts, a_in), (grads, a_out))[i]
        return pltpu.make_async_remote_copy(
            src_ref=source.at[pl.ds(row0, 64), theirs], dst_ref=held.at[pl.ds(TOK + row0, 64)],
            send_sem=y_s.at[i], recv_sem=y_r.at[i], device_id=across, device_id_type=MESH)

    def k_copy(i, first):
        piece = (a_in, a_out)[i].at[pl.ds(TOK + first, 64)]
        return pltpu.make_async_remote_copy(
            src_ref=piece, dst_ref=piece, send_sem=k_s.at[i], recv_sem=k_r.at[i],
            device_id=sibling, device_id_type=MESH)

    def h_copy(i):
        source, target = (psend, precv) if i == 0 else (psends.at[i - 1], precvs.at[i - 1])
        return pltpu.make_async_remote_copy(
            src_ref=source, dst_ref=target, send_sem=h_s.at[i], recv_sem=h_r.at[i],
            device_id=twin, device_id_type=MESH)

    def o_copy(half):
        return pltpu.make_async_remote_copy(
            src_ref=osum.at[half, 1 - h], dst_ref=orecv.at[half], send_sem=o_s.at[half], recv_sem=o_r.at[half],
            device_id=twin, device_id_type=MESH)

    def p_copy(q):
        return pltpu.make_async_remote_copy(
            src_ref=rots.at[q], dst_ref=right.at[z, c // 8], send_sem=p_s.at[q], recv_sem=p_r.at[c // 8],
            device_id={"blk": cz // 2, "pair": lax.rem(cz, 2), "dp": h * NZ + 2 * lax.rem(c, 8) + q},
            device_id_type=MESH)

    def p_arrive(j):
        piece = right.at[zc, j]
        pltpu.make_async_remote_copy(
            src_ref=piece, dst_ref=piece, send_sem=p_s.at[0], recv_sem=p_r.at[j],
            device_id=twin, device_id_type=MESH).wait_recv()

    def q_copy(n, block):
        piece = right.at[block]
        return pltpu.make_async_remote_copy(
            src_ref=piece, dst_ref=piece, send_sem=q_s.at[n], recv_sem=q_r.at[n],
            device_id=peer(*peers[n]), device_id_type=MESH)

    def t_copy(n, block):
        piece = right.at[block]
        return pltpu.make_async_remote_copy(
            src_ref=piece, dst_ref=piece, send_sem=t_s.at[n], recv_sem=t_r.at[n],
            device_id=sibling, device_id_type=MESH)

    def add_in(slot):
        columns = pl.ds(pl.multiple_of(slot * ROWS, ROWS), ROWS)
        acc[...] += jnp.dot(a_in[:, columns], b_in[slot], preferred_element_type=F32)

    def add_out(half, slot):
        columns = pl.ds(pl.multiple_of(slot * ROWS, ROWS), ROWS)
        accs[half] += jnp.dot(a_out[:, columns], b_out[half, slot], preferred_element_type=F32)

    def around(near, far, add):
        @pl.loop(2 * near, 2 * far + 2)
        def _(n):
            add(lax.rem(z + NZ + (2 * lax.rem(n, 2) - 1) * (n // 2), NZ))

    def add_a(slot):
        add_out(0, slot)

    def add_b(slot):
        add_out(1, slot)

    opposite = lax.rem(z + NZ // 2, NZ)

    def square(half, slot):
        left = gath[slot, 0:TOK] if half == 0 else gath2[slot]
        ids = gath[slot, TOK:TOK + TAG].astype(F32)[0:1]
        block = jnp.concatenate([right[slot, 0], right[slot, 1]], axis=1)
        masked = [left * jnp.where(ids == F32(s), F32(1), F32(0)).astype(BF16) for s in range(SEQ_DEV)]
        product = jnp.dot(jnp.concatenate(masked, axis=0), block, preferred_element_type=F32)
        total = None
        for s in range(SEQ_DEV):
            one = product[s * TOK:(s + 1) * TOK]
            total = one * one if total is None else total + one * one
        osum[half, 0] += total[:, :TOK]
        osum[half, 1] += total[:, TOK:]

    def squares(half, r):
        for slot in ring_ga.slots(r):
            square(half, slot)

    def send_partial(half):
        psends[half] = accs[half, TOK:].astype(BF16)
        h_copy(1 + half).start()

    def turned(half):
        h_copy(1 + half).wait_recv()
        return (accs[half, :TOK] + precvs[half].astype(F32)).T.astype(BF16)

    for m in range(LAG_B + 9):
        if m <= 8:
            ring_in.step(m)
        if LAG_A <= m <= LAG_A + 8:
            ring_a.step(m - LAG_A)
        if m >= LAG_B:
            ring_b.step(m - LAG_B)
        if m == 0:
            y_copy(0).start()
            y_copy(1).start()
        if m == 6:
            y_copy(0).wait_recv()
            k_copy(0, row0).start()
        if m == 7:
            loads[2].wait()
            k_copy(0, other0).wait_recv()
            add_in(z)
            around(1, 4, add_in)
            y_copy(1).wait_recv()
            k_copy(1, row0).start()
        if m == 8:
            around(5, 7, add_in)
            add_in(opposite)
            psend[...] = acc[TOK:].astype(BF16)
            h_copy(0).start()
        if m == 9:
            loads[3].wait()
            k_copy(1, other0).wait_recv()
            add_a(z)
            around(1, 6, add_a)
        if m == 10:
            h_copy(0).wait_recv()
            rotated = (acc[:TOK] + precv[...].astype(F32)).astype(BF16)
            rots[0] = rotated[:, :TOK]
            rots[1] = rotated[:, TOK:]
            for q in range(2):
                p_copy(q).start()
            around(7, 7, add_a)
            add_a(opposite)
            send_partial(0)
        if m == 11:
            for j in range(2):
                p_arrive(j)
            for n in range(len(peers)):
                q_copy(n, zc).start()
            t_copy(7, zc).start()
            add_b(z)
            around(1, 5, add_b)
        if m == 12:
            gath[z, 0:TOK] = turned(0)
            ring_ga.round(0)
            for n, (dx, dy) in enumerate(peers):
                block = collected(dx, dy, core)
                q_copy(n, block).wait_recv()
                t_copy(n, block).start()
            around(6, 7, add_b)
        if m == 13:
            add_b(opposite)
            send_partial(1)

    ring_ga.round(1)
    ring_in.finish()
    gath2[z] = turned(1)
    ring_gb.round(0)
    ring_ga.round(2)
    for n, (dx, dy) in enumerate(peers):
        t_copy(n, collected(dx, dy, 1 - core)).wait_recv()
    t_copy(7, collected(0, 0, 1 - core)).wait_recv()
    squares(0, 0)
    squares(0, 1)
    ring_gb.round(1)
    ring_ga.round(3)
    squares(0, 2)
    squares(0, 3)
    ring_gb.round(2)
    ring_ga.round(4)
    squares(0, 4)
    o_copy(0).start()
    squares(1, 0)
    squares(1, 1)
    ring_gb.round(3)
    squares(1, 2)
    for i in range(2):
        y_copy(i).wait_send()
        k_copy(i, row0).wait_send()
        p_copy(i).wait_send()
    for i in range(3):
        h_copy(i).wait_send()
    ring_gb.round(4)
    squares(1, 3)
    squares(1, 4)
    o_copy(1).start()

    for ring in (ring_a, ring_b, ring_ga, ring_gb):
        ring.finish()
    for n, (dx, dy) in enumerate(peers):
        q_copy(n, zc).wait_send()
        t_copy(n, collected(dx, dy, core)).wait_send()
    t_copy(7, zc).wait_send()

    for half in range(2):
        o_copy(half).wait_recv()
        out[half * TOK:(half + 1) * TOK] = (osum[half, h] + orecv[half]) * F32(1.0 / (SEQ_DEV * NZ * NH))
    for half in range(2):
        o_copy(half).wait_send()


def on_device(acts, grads, basis_in, basis_out, seq_ids):
    dma = pltpu.SemaphoreType.DMA
    ring, half, skip = dma((2, 2, 8)), dma((2, 1, 8)), dma((2, 4, 2))
    return pl.pallas_call(
        kernel,
        out_shape=jax.ShapeDtypeStruct((COLS, TOK), F32),
        in_specs=[pl.BlockSpec(memory_space=pl.ANY)] * 4 + [pl.BlockSpec(memory_space=pltpu.VMEM)],
        out_specs=pl.BlockSpec(memory_space=pltpu.VMEM),
        scratch_shapes=[
            pltpu.VMEM((NH * TOK, HALF), BF16),
            pltpu.VMEM((NH * TOK, HALF), BF16),
            pltpu.VMEM((NZ, ROWS, COLS), BF16),
            pltpu.VMEM((2, NZ, ROWS, TOK), BF16),
            pltpu.VMEM((ROWS, COLS), F32),
            pltpu.VMEM((ROWS, COLS), F32),
            pltpu.VMEM((NH * TOK, COLS), F32),
            pltpu.VMEM((2, NH * TOK, TOK), F32),
            pltpu.VMEM((TOK, COLS), BF16),
            pltpu.VMEM((TOK, COLS), BF16),
            pltpu.VMEM((2, TOK, TOK), BF16),
            pltpu.VMEM((2, TOK, TOK), BF16),
            pltpu.VMEM((2, TOK, TOK), BF16),
            pltpu.VMEM((NZ, TOK + TAG, TOK), BF16),
            pltpu.VMEM((NZ, TOK, TOK), BF16),
            pltpu.VMEM((NZ, NH, TOK, TOK), BF16),
            pltpu.VMEM((2, NH, TOK, TOK), F32),
            pltpu.VMEM((2, TOK, TOK), F32),
            dma((4,)),
            ring, ring, half, half, half, half, skip, skip, skip, skip,
            dma((2,)), dma((2,)), dma((2,)), dma((2,)), dma((3,)), dma((3,)),
            dma((2,)), dma((2,)), dma((7,)), dma((7,)), dma((8,)), dma((8,)), dma((2,)), dma((2,)),
        ],
        compiler_params=pltpu.CompilerParams(
            collective_id=0, has_side_effects=True, vmem_limit_bytes=62 * 1024 * 1024),
        cost_estimate=pl.CostEstimate(flops=3_300_000_000, bytes_accessed=8_000_000, transcendentals=0),
    )(acts, grads, basis_in, basis_out, seq_ids.reshape(1, TOK))


def solution(mesh):
    return jax.shard_map(
        on_device,
        mesh=mesh,
        in_specs=(
            P("dp", None),
            P("dp", None),
            P("dp", ("blk", "pair")),
            P("dp", ("blk", "pair")),
            P("dp"),
        ),
        out_specs=P(("blk", "pair"), "dp"),
        check_vma=False,
    )
```

```python
import jax
import jax.numpy as jnp
from jax import lax
from jax.experimental import pallas as pl
from jax.experimental.pallas import tpu as pltpu
from jax.sharding import PartitionSpec as P

SEQ_DEV = 4
TOK = 128
NZ = 16
NH = 2
COLS = 256
ROWS = 256
HALF = NZ * ROWS
LAG_A = 2
LAG_B = 5
TAG = 16
MESH = pl.DeviceIdType.MESH
F32 = jnp.float32
BF16 = jnp.bfloat16


class Ring:
    def __init__(self, piece, hops, send, recv, h, z):
        self.piece, self.hops, self.send, self.recv, self.h, self.z = piece, hops, send, recv, h, z

    def slot(self, way, t):
        return lax.rem(self.z + (NZ - t if way == 0 else t), NZ)

    def copy(self, way, part, t, origin):
        piece = self.piece(part, origin)
        return pltpu.make_async_remote_copy(
            src_ref=piece, dst_ref=piece,
            send_sem=self.send.at[way, part, t], recv_sem=self.recv.at[way, part, t],
            device_id={"dp": self.h * NZ + self.slot(1 - way, 1)}, device_id_type=MESH)

    def step(self, s):
        for part in range(len(self.hops)):
            for way in range(2):
                hops = self.hops[part][way]
                if 1 <= s <= hops:
                    self.copy(way, part, s - 1, self.slot(way, s)).wait_recv()
                if s < hops:
                    self.copy(way, part, s, self.slot(way, s)).start()

    def finish(self):
        for part in range(len(self.hops)):
            for way in range(2):
                for t in range(self.hops[part][way]):
                    self.copy(way, part, t, self.slot(way, t)).wait_send()


class Skip:
    def __init__(self, piece, hops, send, recv, h, z):
        self.piece, self.hops, self.send, self.recv, self.h, self.z = piece, hops, send, recv, h, z

    def slot(self, way, t):
        return lax.rem(self.z + (NZ - t if way == 0 else t), NZ)

    def copy(self, way, r, far, origin):
        piece = self.piece(origin)
        return pltpu.make_async_remote_copy(
            src_ref=piece, dst_ref=piece,
            send_sem=self.send.at[way, r, far], recv_sem=self.recv.at[way, r, far],
            device_id={"dp": self.h * NZ + self.slot(1 - way, 1 + far)}, device_id_type=MESH)

    def round(self, r):
        for way in range(2):
            if r >= 1 and 2 * r <= self.hops[way]:
                self.copy(way, r - 1, 1, self.slot(way, 2 * r)).wait_recv()
            if r < 4:
                for far in (1, 0):
                    if 2 * r + 1 + far <= self.hops[way]:
                        self.copy(way, r, far, self.slot(way, 2 * r)).start()
        if r >= 1:
            for way in range(2):
                self.copy(way, r - 1, 0, self.slot(way, 2 * r - 1)).wait_recv()

    def slots(self, r):
        if r == 0:
            return [self.z]
        near = [self.slot(0, 2 * r - 1), self.slot(1, 2 * r - 1), self.slot(0, 2 * r)]
        return near if r == 4 else near + [self.slot(1, 2 * r)]

    def finish(self):
        for way in range(2):
            for r in range(4):
                for far in range(2):
                    if 2 * r + 1 + far <= self.hops[way]:
                        self.copy(way, r, far, self.slot(way, 2 * r)).wait_send()


def kernel(acts, grads, basis_in, basis_out, seq, out,
           a_in, a_out, b_in, b_out, f_in, f_out, acc, accs, psend, precv, psends, precvs, rots, gath, gath2, right,
           osum, orecv,
           load, in_s, in_r, out_s, out_r, out2_s, out2_r, g_s, g_r, g2_s, g2_r,
           y_s, y_r, k_s, k_r, h_s, h_r, p_s, p_r, q_s, q_r, t_s, t_r, o_s, o_r):
    blk, pair, dp = lax.axis_index("blk"), lax.axis_index("pair"), lax.axis_index("dp")
    x, core = blk // 2, lax.rem(blk, 2)
    h, z = dp // NZ, lax.rem(dp, NZ)
    c = blk * 2 + pair
    zc = lax.rem(c + z // 2 + NZ - 2, NZ)
    cz = lax.rem(z - lax.rem(c, 8) + 2 + NZ, NZ)
    row0 = pl.multiple_of(core * 64, 64)
    other0 = pl.multiple_of((1 - core) * 64, 64)

    across = {"pair": 1 - pair, "dp": (1 - h) * NZ + z}
    twin = {"dp": (1 - h) * NZ + z}
    sibling = {"blk": x * 2 + 1 - core}
    peers = [(dx, dy) for dx in range(4) for dy in range(2) if (dx, dy) != (0, 0)]

    def peer(dx, dy):
        return {"blk": lax.rem(x + dx, 4) * 2 + core, "pair": lax.rem(pair + dy, 2)}

    def collected(dx, dy, k):
        of = (lax.rem(x - dx + 4, 4) * 2 + k) * 2 + lax.rem(pair + dy, 2)
        return lax.rem(of + z // 2 + NZ - 2, NZ)

    mine = pl.ds(pl.multiple_of(h * HALF, HALF), HALF)
    theirs = pl.ds(pl.multiple_of((1 - h) * HALF, HALF), HALF)
    loads = [
        pltpu.make_async_copy(basis_in, f_in, load.at[0]),
        pltpu.make_async_copy(basis_out, f_out, load.at[1]),
        pltpu.make_async_copy(acts.at[:, mine], a_in.at[pl.ds(0, TOK)], load.at[2]),
        pltpu.make_async_copy(grads.at[:, mine], a_out.at[pl.ds(0, TOK)], load.at[3]),
    ]
    for one in loads:
        one.start()

    barrier = pltpu.get_barrier_semaphore()
    greet = [
        {"dp": h * NZ + lax.rem(z + 1, NZ)},
        {"dp": h * NZ + lax.rem(z + NZ - 1, NZ)},
        {"dp": h * NZ + lax.rem(z + 2, NZ)},
        {"dp": h * NZ + lax.rem(z + NZ - 2, NZ)},
        across, twin, sibling,
        {"blk": (z // 2) // 2, "pair": lax.rem(z // 2, 2), "dp": h * NZ + zc},
        {"blk": (z // 2) // 2 + 4, "pair": lax.rem(z // 2, 2), "dp": h * NZ + zc},
    ] + [peer(dx, dy) for dx, dy in peers]
    for device in greet:
        pl.semaphore_signal(barrier, inc=1, device_id=device, device_id_type=MESH)

    loads[0].wait()
    b_in[z] = f_in[...].astype(BF16)
    loads[1].wait()
    b_out[0, z] = f_out[:, :TOK].astype(BF16)
    b_out[1, z] = f_out[:, TOK:].astype(BF16)
    tags = jnp.bitwise_and(seq[...], SEQ_DEV - 1).astype(F32)
    gath[z, TOK:TOK + TAG] = jnp.broadcast_to(tags, (TAG, TOK)).astype(BF16)
    osum[...] = jnp.zeros_like(osum)
    acc[...] = jnp.zeros_like(acc)
    accs[...] = jnp.zeros_like(accs)

    pl.semaphore_wait(barrier, len(greet))

    part_rows = ROWS // 2
    ring_in = Ring(lambda part, slot: b_in.at[slot, pl.ds(part * part_rows, part_rows)],
                   ((8, 7), (7, 8)), in_s, in_r, h, z)
    ring_a = Ring(lambda part, slot: b_out.at[0, slot], ((8, 7),), out_s, out_r, h, z)
    ring_b = Ring(lambda part, slot: b_out.at[1, slot], ((7, 8),), out2_s, out2_r, h, z)
    ring_ga = Skip(lambda slot: gath.at[slot], (8, 7), g_s, g_r, h, z)
    ring_gb = Skip(lambda slot: gath2.at[slot], (7, 8), g2_s, g2_r, h, z)

    def y_copy(i):
        source, held = ((acts, a_in), (grads, a_out))[i]
        return pltpu.make_async_remote_copy(
            src_ref=source.at[pl.ds(row0, 64), theirs], dst_ref=held.at[pl.ds(TOK + row0, 64)],
            send_sem=y_s.at[i], recv_sem=y_r.at[i], device_id=across, device_id_type=MESH)

    def k_copy(i, first):
        piece = (a_in, a_out)[i].at[pl.ds(TOK + first, 64)]
        return pltpu.make_async_remote_copy(
            src_ref=piece, dst_ref=piece, send_sem=k_s.at[i], recv_sem=k_r.at[i],
            device_id=sibling, device_id_type=MESH)

    def h_copy(i):
        source, target = (psend, precv) if i == 0 else (psends.at[i - 1], precvs.at[i - 1])
        return pltpu.make_async_remote_copy(
            src_ref=source, dst_ref=target, send_sem=h_s.at[i], recv_sem=h_r.at[i],
            device_id=twin, device_id_type=MESH)

    def o_copy(half):
        return pltpu.make_async_remote_copy(
            src_ref=osum.at[half, 1 - h], dst_ref=orecv.at[half], send_sem=o_s.at[half], recv_sem=o_r.at[half],
            device_id=twin, device_id_type=MESH)

    def p_copy(q):
        return pltpu.make_async_remote_copy(
            src_ref=rots.at[q], dst_ref=right.at[z, c // 8], send_sem=p_s.at[q], recv_sem=p_r.at[c // 8],
            device_id={"blk": cz // 2, "pair": lax.rem(cz, 2), "dp": h * NZ + 2 * lax.rem(c, 8) + q},
            device_id_type=MESH)

    def p_arrive(j):
        piece = right.at[zc, j]
        pltpu.make_async_remote_copy(
            src_ref=piece, dst_ref=piece, send_sem=p_s.at[0], recv_sem=p_r.at[j],
            device_id=twin, device_id_type=MESH).wait_recv()

    def q_copy(n, block):
        piece = right.at[block]
        return pltpu.make_async_remote_copy(
            src_ref=piece, dst_ref=piece, send_sem=q_s.at[n], recv_sem=q_r.at[n],
            device_id=peer(*peers[n]), device_id_type=MESH)

    def t_copy(n, block):
        piece = right.at[block]
        return pltpu.make_async_remote_copy(
            src_ref=piece, dst_ref=piece, send_sem=t_s.at[n], recv_sem=t_r.at[n],
            device_id=sibling, device_id_type=MESH)

    def add_in(slot):
        columns = pl.ds(pl.multiple_of(slot * ROWS, ROWS), ROWS)
        acc[...] += jnp.dot(a_in[:, columns], b_in[slot], preferred_element_type=F32)

    def add_out(half, slot):
        columns = pl.ds(pl.multiple_of(slot * ROWS, ROWS), ROWS)
        accs[half] += jnp.dot(a_out[:, columns], b_out[half, slot], preferred_element_type=F32)

    def around(near, far, add):
        @pl.loop(2 * near, 2 * far + 2)
        def _(n):
            add(lax.rem(z + NZ + (2 * lax.rem(n, 2) - 1) * (n // 2), NZ))

    def add_a(slot):
        add_out(0, slot)

    def add_b(slot):
        add_out(1, slot)

    opposite = lax.rem(z + NZ // 2, NZ)

    def square(half, slot):
        left = gath[slot, 0:TOK] if half == 0 else gath2[slot]
        ids = gath[slot, TOK:TOK + TAG].astype(F32)[0:1]
        block = jnp.concatenate([right[slot, 0], right[slot, 1]], axis=1)
        masked = [left * jnp.where(ids == F32(s), F32(1), F32(0)).astype(BF16) for s in range(SEQ_DEV)]
        product = jnp.dot(jnp.concatenate(masked, axis=0), block, preferred_element_type=F32)
        total = None
        for s in range(SEQ_DEV):
            one = product[s * TOK:(s + 1) * TOK]
            total = one * one if total is None else total + one * one
        osum[half, 0] += total[:, :TOK]
        osum[half, 1] += total[:, TOK:]

    def squares(half, r):
        for slot in ring_ga.slots(r):
            square(half, slot)

    def send_partial(half):
        psends[half] = accs[half, TOK:].astype(BF16)
        h_copy(1 + half).start()

    def turned(half):
        h_copy(1 + half).wait_recv()
        return (accs[half, :TOK] + precvs[half].astype(F32)).T.astype(BF16)

    for m in range(LAG_B + 9):
        if m <= 8:
            ring_in.step(m)
        if LAG_A <= m <= LAG_A + 8:
            ring_a.step(m - LAG_A)
        if m >= LAG_B:
            ring_b.step(m - LAG_B)
        if m == 0:
            y_copy(0).start()
            y_copy(1).start()
        if m == 6:
            y_copy(0).wait_recv()
            k_copy(0, row0).start()
        if m == 7:
            loads[2].wait()
            k_copy(0, other0).wait_recv()
            add_in(z)
            around(1, 4, add_in)
            y_copy(1).wait_recv()
            k_copy(1, row0).start()
        if m == 8:
            around(5, 7, add_in)
            add_in(opposite)
            psend[...] = acc[TOK:].astype(BF16)
            h_copy(0).start()
        if m == 9:
            loads[3].wait()
            k_copy(1, other0).wait_recv()
            add_a(z)
            around(1, 6, add_a)
            h_copy(0).wait_recv()
            rotated = (acc[:TOK] + precv[...].astype(F32)).astype(BF16)
            rots[0] = rotated[:, :TOK]
            rots[1] = rotated[:, TOK:]
            for q in range(2):
                p_copy(q).start()
        if m == 10:
            around(7, 7, add_a)
            add_a(opposite)
            send_partial(0)
        if m == 11:
            add_b(z)
            around(1, 5, add_b)
            for j in range(2):
                p_arrive(j)
            for n in range(len(peers)):
                q_copy(n, zc).start()
            t_copy(7, zc).start()
        if m == 12:
            gath[z, 0:TOK] = turned(0)
            ring_ga.round(0)
            around(6, 7, add_b)
        if m == 13:
            add_b(opposite)
            send_partial(1)

    ring_ga.round(1)
    ring_in.finish()
    gath2[z] = turned(1)
    ring_gb.round(0)
    ring_ga.round(2)
    for n, (dx, dy) in enumerate(peers):
        block = collected(dx, dy, core)
        q_copy(n, block).wait_recv()
        t_copy(n, block).start()
    ring_gb.round(1)
    ring_ga.round(3)
    for n, (dx, dy) in enumerate(peers):
        t_copy(n, collected(dx, dy, 1 - core)).wait_recv()
    t_copy(7, collected(0, 0, 1 - core)).wait_recv()
    squares(0, 0)
    squares(0, 1)
    squares(0, 2)
    ring_gb.round(2)
    ring_ga.round(4)
    squares(0, 3)
    squares(0, 4)
    o_copy(0).start()
    squares(1, 0)
    squares(1, 1)
    ring_gb.round(3)
    squares(1, 2)
    for i in range(2):
        y_copy(i).wait_send()
        k_copy(i, row0).wait_send()
        p_copy(i).wait_send()
    for i in range(3):
        h_copy(i).wait_send()
    ring_gb.round(4)
    squares(1, 3)
    squares(1, 4)
    o_copy(1).start()

    for ring in (ring_a, ring_b, ring_ga, ring_gb):
        ring.finish()
    for n, (dx, dy) in enumerate(peers):
        q_copy(n, zc).wait_send()
        t_copy(n, collected(dx, dy, core)).wait_send()
    t_copy(7, zc).wait_send()

    for half in range(2):
        o_copy(half).wait_recv()
        out[half * TOK:(half + 1) * TOK] = (osum[half, h] + orecv[half]) * F32(1.0 / (SEQ_DEV * NZ * NH))
    for half in range(2):
        o_copy(half).wait_send()


def on_device(acts, grads, basis_in, basis_out, seq_ids):
    dma = pltpu.SemaphoreType.DMA
    ring, half, skip = dma((2, 2, 8)), dma((2, 1, 8)), dma((2, 4, 2))
    return pl.pallas_call(
        kernel,
        out_shape=jax.ShapeDtypeStruct((COLS, TOK), F32),
        in_specs=[pl.BlockSpec(memory_space=pl.ANY)] * 4 + [pl.BlockSpec(memory_space=pltpu.VMEM)],
        out_specs=pl.BlockSpec(memory_space=pltpu.VMEM),
        scratch_shapes=[
            pltpu.VMEM((NH * TOK, HALF), BF16),
            pltpu.VMEM((NH * TOK, HALF), BF16),
            pltpu.VMEM((NZ, ROWS, COLS), BF16),
            pltpu.VMEM((2, NZ, ROWS, TOK), BF16),
            pltpu.VMEM((ROWS, COLS), F32),
            pltpu.VMEM((ROWS, COLS), F32),
            pltpu.VMEM((NH * TOK, COLS), F32),
            pltpu.VMEM((2, NH * TOK, TOK), F32),
            pltpu.VMEM((TOK, COLS), BF16),
            pltpu.VMEM((TOK, COLS), BF16),
            pltpu.VMEM((2, TOK, TOK), BF16),
            pltpu.VMEM((2, TOK, TOK), BF16),
            pltpu.VMEM((2, TOK, TOK), BF16),
            pltpu.VMEM((NZ, TOK + TAG, TOK), BF16),
            pltpu.VMEM((NZ, TOK, TOK), BF16),
            pltpu.VMEM((NZ, NH, TOK, TOK), BF16),
            pltpu.VMEM((2, NH, TOK, TOK), F32),
            pltpu.VMEM((2, TOK, TOK), F32),
            dma((4,)),
            ring, ring, half, half, half, half, skip, skip, skip, skip,
            dma((2,)), dma((2,)), dma((2,)), dma((2,)), dma((3,)), dma((3,)),
            dma((2,)), dma((2,)), dma((7,)), dma((7,)), dma((8,)), dma((8,)), dma((2,)), dma((2,)),
        ],
        compiler_params=pltpu.CompilerParams(
            collective_id=0, has_side_effects=True, vmem_limit_bytes=62 * 1024 * 1024),
        cost_estimate=pl.CostEstimate(flops=3_300_000_000, bytes_accessed=8_000_000, transcendentals=0),
    )(acts, grads, basis_in, basis_out, seq_ids.reshape(1, TOK))


def solution(mesh):
    return jax.shard_map(
        on_device,
        mesh=mesh,
        in_specs=(
            P("dp", None),
            P("dp", None),
            P("dp", ("blk", "pair")),
            P("dp", ("blk", "pair")),
            P("dp"),
        ),
        out_specs=P(("blk", "pair"), "dp"),
        check_vma=False,
    )
```

```python
import jax
import jax.numpy as jnp
from jax import lax
from jax.experimental import pallas as pl
from jax.experimental.pallas import tpu as pltpu
from jax.sharding import PartitionSpec as P

SEQ_DEV = 4
TOK = 128
NZ = 16
NH = 2
COLS = 256
ROWS = 256
HALF = NZ * ROWS
LAG_A = 2
LAG_B = 5
TAG = 16
MESH = pl.DeviceIdType.MESH
F32 = jnp.float32
BF16 = jnp.bfloat16


class Ring:
    def __init__(self, piece, hops, send, recv, h, z):
        self.piece, self.hops, self.send, self.recv, self.h, self.z = piece, hops, send, recv, h, z

    def slot(self, way, t):
        return lax.rem(self.z + (NZ - t if way == 0 else t), NZ)

    def copy(self, way, part, t, origin):
        piece = self.piece(part, origin)
        return pltpu.make_async_remote_copy(
            src_ref=piece, dst_ref=piece,
            send_sem=self.send.at[way, part, t], recv_sem=self.recv.at[way, part, t],
            device_id={"dp": self.h * NZ + self.slot(1 - way, 1)}, device_id_type=MESH)

    def step(self, s):
        for part in range(len(self.hops)):
            for way in range(2):
                hops = self.hops[part][way]
                if 1 <= s <= hops:
                    self.copy(way, part, s - 1, self.slot(way, s)).wait_recv()
                if s < hops:
                    self.copy(way, part, s, self.slot(way, s)).start()

    def finish(self):
        for part in range(len(self.hops)):
            for way in range(2):
                for t in range(self.hops[part][way]):
                    self.copy(way, part, t, self.slot(way, t)).wait_send()


class Skip:
    def __init__(self, piece, hops, send, recv, h, z):
        self.piece, self.hops, self.send, self.recv, self.h, self.z = piece, hops, send, recv, h, z

    def slot(self, way, t):
        return lax.rem(self.z + (NZ - t if way == 0 else t), NZ)

    def copy(self, way, r, far, origin):
        piece = self.piece(origin)
        return pltpu.make_async_remote_copy(
            src_ref=piece, dst_ref=piece,
            send_sem=self.send.at[way, r, far], recv_sem=self.recv.at[way, r, far],
            device_id={"dp": self.h * NZ + self.slot(1 - way, 1 + far)}, device_id_type=MESH)

    def round(self, r):
        for way in range(2):
            if r >= 1 and 2 * r <= self.hops[way]:
                self.copy(way, r - 1, 1, self.slot(way, 2 * r)).wait_recv()
            if r < 4:
                for far in (1, 0):
                    if 2 * r + 1 + far <= self.hops[way]:
                        self.copy(way, r, far, self.slot(way, 2 * r)).start()
        if r >= 1:
            for way in range(2):
                self.copy(way, r - 1, 0, self.slot(way, 2 * r - 1)).wait_recv()

    def slots(self, r):
        if r == 0:
            return [self.z]
        near = [self.slot(0, 2 * r - 1), self.slot(1, 2 * r - 1), self.slot(0, 2 * r)]
        return near if r == 4 else near + [self.slot(1, 2 * r)]

    def finish(self):
        for way in range(2):
            for r in range(4):
                for far in range(2):
                    if 2 * r + 1 + far <= self.hops[way]:
                        self.copy(way, r, far, self.slot(way, 2 * r)).wait_send()


def kernel(acts, grads, basis_in, basis_out, seq, out,
           a_in, a_out, b_in, b_out, f_in, f_out, acc, accs, psend, precv, psends, precvs, rots, gath, gath2, right,
           osum, orecv,
           load, in_s, in_r, out_s, out_r, out2_s, out2_r, g_s, g_r, g2_s, g2_r,
           y_s, y_r, k_s, k_r, h_s, h_r, p_s, p_r, q_s, q_r, t_s, t_r, o_s, o_r):
    blk, pair, dp = lax.axis_index("blk"), lax.axis_index("pair"), lax.axis_index("dp")
    x, core = blk // 2, lax.rem(blk, 2)
    h, z = dp // NZ, lax.rem(dp, NZ)
    c = blk * 2 + pair
    zc = lax.rem(c + z // 2 + NZ - 2, NZ)
    cz = lax.rem(z - lax.rem(c, 8) + 2 + NZ, NZ)
    row0 = pl.multiple_of(core * 64, 64)
    other0 = pl.multiple_of((1 - core) * 64, 64)

    across = {"pair": 1 - pair, "dp": (1 - h) * NZ + z}
    twin = {"dp": (1 - h) * NZ + z}
    sibling = {"blk": x * 2 + 1 - core}
    peers = [(dx, dy) for dx in range(4) for dy in range(2) if (dx, dy) != (0, 0)]

    def peer(dx, dy):
        return {"blk": lax.rem(x + dx, 4) * 2 + core, "pair": lax.rem(pair + dy, 2)}

    def collected(dx, dy, k):
        of = (lax.rem(x - dx + 4, 4) * 2 + k) * 2 + lax.rem(pair + dy, 2)
        return lax.rem(of + z // 2 + NZ - 2, NZ)

    mine = pl.ds(pl.multiple_of(h * HALF, HALF), HALF)
    theirs = pl.ds(pl.multiple_of((1 - h) * HALF, HALF), HALF)
    loads = [
        pltpu.make_async_copy(basis_in, f_in, load.at[0]),
        pltpu.make_async_copy(basis_out, f_out, load.at[1]),
        pltpu.make_async_copy(acts.at[:, mine], a_in.at[pl.ds(0, TOK)], load.at[2]),
        pltpu.make_async_copy(grads.at[:, mine], a_out.at[pl.ds(0, TOK)], load.at[3]),
    ]
    for one in loads:
        one.start()

    barrier = pltpu.get_barrier_semaphore()
    greet = [
        {"dp": h * NZ + lax.rem(z + 1, NZ)},
        {"dp": h * NZ + lax.rem(z + NZ - 1, NZ)},
        {"dp": h * NZ + lax.rem(z + 2, NZ)},
        {"dp": h * NZ + lax.rem(z + NZ - 2, NZ)},
        across, twin, sibling,
        {"blk": (z // 2) // 2, "pair": lax.rem(z // 2, 2), "dp": h * NZ + zc},
        {"blk": (z // 2) // 2 + 4, "pair": lax.rem(z // 2, 2), "dp": h * NZ + zc},
    ] + [peer(dx, dy) for dx, dy in peers]
    for device in greet:
        pl.semaphore_signal(barrier, inc=1, device_id=device, device_id_type=MESH)

    loads[0].wait()
    b_in[z] = f_in[...].astype(BF16)
    loads[1].wait()
    b_out[0, z] = f_out[:, :TOK].astype(BF16)
    b_out[1, z] = f_out[:, TOK:].astype(BF16)
    tags = jnp.bitwise_and(seq[...], SEQ_DEV - 1).astype(F32)
    gath[z, TOK:TOK + TAG] = jnp.broadcast_to(tags, (TAG, TOK)).astype(BF16)
    osum[...] = jnp.zeros_like(osum)
    acc[...] = jnp.zeros_like(acc)
    accs[...] = jnp.zeros_like(accs)

    pl.semaphore_wait(barrier, len(greet))

    part_rows = ROWS // 2
    ring_in = Ring(lambda part, slot: b_in.at[slot, pl.ds(part * part_rows, part_rows)],
                   ((8, 7), (7, 8)), in_s, in_r, h, z)
    ring_a = Ring(lambda part, slot: b_out.at[0, slot], ((8, 7),), out_s, out_r, h, z)
    ring_b = Ring(lambda part, slot: b_out.at[1, slot], ((7, 8),), out2_s, out2_r, h, z)
    ring_ga = Skip(lambda slot: gath.at[slot], (8, 7), g_s, g_r, h, z)
    ring_gb = Skip(lambda slot: gath2.at[slot], (7, 8), g2_s, g2_r, h, z)

    def y_copy(i):
        source, held = ((acts, a_in), (grads, a_out))[i]
        return pltpu.make_async_remote_copy(
            src_ref=source.at[pl.ds(row0, 64), theirs], dst_ref=held.at[pl.ds(TOK + row0, 64)],
            send_sem=y_s.at[i], recv_sem=y_r.at[i], device_id=across, device_id_type=MESH)

    def k_copy(i, first):
        piece = (a_in, a_out)[i].at[pl.ds(TOK + first, 64)]
        return pltpu.make_async_remote_copy(
            src_ref=piece, dst_ref=piece, send_sem=k_s.at[i], recv_sem=k_r.at[i],
            device_id=sibling, device_id_type=MESH)

    def h_copy(i):
        source, target = (psend, precv) if i == 0 else (psends.at[i - 1], precvs.at[i - 1])
        return pltpu.make_async_remote_copy(
            src_ref=source, dst_ref=target, send_sem=h_s.at[i], recv_sem=h_r.at[i],
            device_id=twin, device_id_type=MESH)

    def o_copy(half):
        return pltpu.make_async_remote_copy(
            src_ref=osum.at[half, 1 - h], dst_ref=orecv.at[half], send_sem=o_s.at[half], recv_sem=o_r.at[half],
            device_id=twin, device_id_type=MESH)

    def p_copy(q):
        return pltpu.make_async_remote_copy(
            src_ref=rots.at[q], dst_ref=right.at[z, c // 8], send_sem=p_s.at[q], recv_sem=p_r.at[c // 8],
            device_id={"blk": cz // 2, "pair": lax.rem(cz, 2), "dp": h * NZ + 2 * lax.rem(c, 8) + q},
            device_id_type=MESH)

    def p_arrive(j):
        piece = right.at[zc, j]
        pltpu.make_async_remote_copy(
            src_ref=piece, dst_ref=piece, send_sem=p_s.at[0], recv_sem=p_r.at[j],
            device_id=twin, device_id_type=MESH).wait_recv()

    def q_copy(n, block):
        piece = right.at[block]
        return pltpu.make_async_remote_copy(
            src_ref=piece, dst_ref=piece, send_sem=q_s.at[n], recv_sem=q_r.at[n],
            device_id=peer(*peers[n]), device_id_type=MESH)

    def t_copy(n, block):
        piece = right.at[block]
        return pltpu.make_async_remote_copy(
            src_ref=piece, dst_ref=piece, send_sem=t_s.at[n], recv_sem=t_r.at[n],
            device_id=sibling, device_id_type=MESH)

    def add_in(slot):
        columns = pl.ds(pl.multiple_of(slot * ROWS, ROWS), ROWS)
        acc[...] += jnp.dot(a_in[:, columns], b_in[slot], preferred_element_type=F32)

    def add_out(half, slot):
        columns = pl.ds(pl.multiple_of(slot * ROWS, ROWS), ROWS)
        accs[half] += jnp.dot(a_out[:, columns], b_out[half, slot], preferred_element_type=F32)

    def around(near, far, add):
        @pl.loop(2 * near, 2 * far + 2)
        def _(n):
            add(lax.rem(z + NZ + (2 * lax.rem(n, 2) - 1) * (n // 2), NZ))

    def add_a(slot):
        add_out(0, slot)

    def add_b(slot):
        add_out(1, slot)

    opposite = lax.rem(z + NZ // 2, NZ)

    def square(half, slot):
        left = gath[slot, 0:TOK] if half == 0 else gath2[slot]
        ids = gath[slot, TOK:TOK + TAG].astype(F32)[0:1]
        block = jnp.concatenate([right[slot, 0], right[slot, 1]], axis=1)
        masked = [left * jnp.where(ids == F32(s), F32(1), F32(0)).astype(BF16) for s in range(SEQ_DEV)]
        product = jnp.dot(jnp.concatenate(masked, axis=0), block, preferred_element_type=F32)
        total = None
        for s in range(SEQ_DEV):
            one = product[s * TOK:(s + 1) * TOK]
            total = one * one if total is None else total + one * one
        osum[half, 0] += total[:, :TOK]
        osum[half, 1] += total[:, TOK:]

    def squares(half, r):
        for slot in ring_ga.slots(r):
            square(half, slot)

    def send_partial(half):
        psends[half] = accs[half, TOK:].astype(BF16)
        h_copy(1 + half).start()

    def turned(half):
        h_copy(1 + half).wait_recv()
        return (accs[half, :TOK] + precvs[half].astype(F32)).T.astype(BF16)

    for m in range(LAG_B + 9):
        if m <= 8:
            ring_in.step(m)
        if LAG_A <= m <= LAG_A + 8:
            ring_a.step(m - LAG_A)
        if m >= LAG_B:
            ring_b.step(m - LAG_B)
        if m == 0:
            y_copy(0).start()
            y_copy(1).start()
        if m == 6:
            y_copy(0).wait_recv()
            k_copy(0, row0).start()
        if m == 7:
            loads[2].wait()
            k_copy(0, other0).wait_recv()
            add_in(z)
            around(1, 4, add_in)
            y_copy(1).wait_recv()
            k_copy(1, row0).start()
        if m == 8:
            around(5, 7, add_in)
            add_in(opposite)
            psend[...] = acc[TOK:].astype(BF16)
            h_copy(0).start()
        if m == 9:
            loads[3].wait()
            k_copy(1, other0).wait_recv()
            add_a(z)
            around(1, 6, add_a)
            h_copy(0).wait_recv()
            rotated = (acc[:TOK] + precv[...].astype(F32)).astype(BF16)
            rots[0] = rotated[:, :TOK]
            rots[1] = rotated[:, TOK:]
            for q in range(2):
                p_copy(q).start()
        if m == 10:
            around(7, 7, add_a)
            add_a(opposite)
            send_partial(0)
        if m == 11:
            add_b(z)
            around(1, 5, add_b)
            for j in range(2):
                p_arrive(j)
            for n in range(len(peers)):
                q_copy(n, zc).start()
            t_copy(7, zc).start()
        if m == 12:
            gath[z, 0:TOK] = turned(0)
            ring_ga.round(0)
            around(6, 7, add_b)
        if m == 13:
            add_b(opposite)
            send_partial(1)

    ring_ga.round(1)
    for ring in (ring_in, ring_a, ring_b):
        ring.finish()
    gath2[z] = turned(1)
    ring_gb.round(0)
    ring_ga.round(2)
    for n, (dx, dy) in enumerate(peers):
        block = collected(dx, dy, core)
        q_copy(n, block).wait_recv()
        t_copy(n, block).start()
    ring_gb.round(1)
    ring_ga.round(3)
    for n, (dx, dy) in enumerate(peers):
        t_copy(n, collected(dx, dy, 1 - core)).wait_recv()
    t_copy(7, collected(0, 0, 1 - core)).wait_recv()
    squares(0, 0)
    squares(0, 1)
    squares(0, 2)
    ring_gb.round(2)
    ring_ga.round(4)
    squares(0, 3)
    squares(0, 4)
    o_copy(0).start()
    squares(1, 0)
    squares(1, 1)
    ring_gb.round(3)
    squares(1, 2)
    squares(1, 3)
    for i in range(2):
        y_copy(i).wait_send()
        k_copy(i, row0).wait_send()
        p_copy(i).wait_send()
    for i in range(3):
        h_copy(i).wait_send()
    ring_gb.round(4)
    squares(1, 4)
    o_copy(1).start()

    for ring in (ring_ga, ring_gb):
        ring.finish()
    for n, (dx, dy) in enumerate(peers):
        q_copy(n, zc).wait_send()
        t_copy(n, collected(dx, dy, core)).wait_send()
    t_copy(7, zc).wait_send()

    for half in range(2):
        o_copy(half).wait_recv()
        out[half * TOK:(half + 1) * TOK] = (osum[half, h] + orecv[half]) * F32(1.0 / (SEQ_DEV * NZ * NH))
    for half in range(2):
        o_copy(half).wait_send()


def on_device(acts, grads, basis_in, basis_out, seq_ids):
    dma = pltpu.SemaphoreType.DMA
    ring, half, skip = dma((2, 2, 8)), dma((2, 1, 8)), dma((2, 4, 2))
    return pl.pallas_call(
        kernel,
        out_shape=jax.ShapeDtypeStruct((COLS, TOK), F32),
        in_specs=[pl.BlockSpec(memory_space=pl.ANY)] * 4 + [pl.BlockSpec(memory_space=pltpu.VMEM)],
        out_specs=pl.BlockSpec(memory_space=pltpu.VMEM),
        scratch_shapes=[
            pltpu.VMEM((NH * TOK, HALF), BF16),
            pltpu.VMEM((NH * TOK, HALF), BF16),
            pltpu.VMEM((NZ, ROWS, COLS), BF16),
            pltpu.VMEM((2, NZ, ROWS, TOK), BF16),
            pltpu.VMEM((ROWS, COLS), F32),
            pltpu.VMEM((ROWS, COLS), F32),
            pltpu.VMEM((NH * TOK, COLS), F32),
            pltpu.VMEM((2, NH * TOK, TOK), F32),
            pltpu.VMEM((TOK, COLS), BF16),
            pltpu.VMEM((TOK, COLS), BF16),
            pltpu.VMEM((2, TOK, TOK), BF16),
            pltpu.VMEM((2, TOK, TOK), BF16),
            pltpu.VMEM((2, TOK, TOK), BF16),
            pltpu.VMEM((NZ, TOK + TAG, TOK), BF16),
            pltpu.VMEM((NZ, TOK, TOK), BF16),
            pltpu.VMEM((NZ, NH, TOK, TOK), BF16),
            pltpu.VMEM((2, NH, TOK, TOK), F32),
            pltpu.VMEM((2, TOK, TOK), F32),
            dma((4,)),
            ring, ring, half, half, half, half, skip, skip, skip, skip,
            dma((2,)), dma((2,)), dma((2,)), dma((2,)), dma((3,)), dma((3,)),
            dma((2,)), dma((2,)), dma((7,)), dma((7,)), dma((8,)), dma((8,)), dma((2,)), dma((2,)),
        ],
        compiler_params=pltpu.CompilerParams(
            collective_id=0, has_side_effects=True, vmem_limit_bytes=62 * 1024 * 1024),
        cost_estimate=pl.CostEstimate(flops=3_300_000_000, bytes_accessed=8_000_000, transcendentals=0),
    )(acts, grads, basis_in, basis_out, seq_ids.reshape(1, TOK))


def solution(mesh):
    return jax.shard_map(
        on_device,
        mesh=mesh,
        in_specs=(
            P("dp", None),
            P("dp", None),
            P("dp", ("blk", "pair")),
            P("dp", ("blk", "pair")),
            P("dp"),
        ),
        out_specs=P(("blk", "pair"), "dp"),
        check_vma=False,
    )
```
